32 devices in a mesh: groups: 2 (over y), pool: 4 (over z), tensor: 4 (over x, core).
Axes of the slice: x: 2, y: 2, z: 4, core: 2. Of those that a mesh axis runs over, the one named last changes fastest.
Arguments:
- incoming_hidden: bfloat16 [4, 8, 8192], P(None, ('groups', 'pool')), parts along dimension 1, may hold values from -6 to 6
- attention_norm_gain: bfloat16 [8192], replicated, may hold values from 0.099609375 to 1.8984375
- frozen_query_weight: bfloat16 [8192, 8192], P('pool', 'tensor'), may hold values from -0.0625 to 0.0625
- frozen_key_weight: bfloat16 [8192, 1024], P('pool', 'tensor'), may hold values from -0.0625 to 0.0625
- frozen_value_weight: bfloat16 [8192, 1024], P('pool', 'tensor'), may hold values from -0.0625 to 0.0625
- frozen_output_weight: bfloat16 [8192, 8192], P('tensor', 'pool'), may hold values from -1 to 1
- query_adapter_first: bfloat16 [16384, 64], P('groups', 'pool'), parts along dimension 0, may hold values from -0.0625 to 0.0625
- query_adapter_second: bfloat16 [128, 8192], P(('groups', 'pool')), parts along dimension 0, may hold values from -0.75 to 0.75
- key_adapter_first: bfloat16 [16384, 64], P('groups', 'pool'), parts along dimension 0, may hold values from -0.0625 to 0.0625
- key_adapter_second: bfloat16 [128, 1024], P(('groups', 'pool')), parts along dimension 0, may hold values from -0.75 to 0.75
- value_adapter_first: bfloat16 [16384, 64], P('groups', 'pool'), parts along dimension 0, may hold values from -0.0625 to 0.0625
- value_adapter_second: bfloat16 [128, 1024], P(('groups', 'pool')), parts along dimension 0, may hold values from -0.75 to 0.75
- output_adapter_first: bfloat16 [16384, 64], P('groups', 'pool'), parts along dimension 0, may hold values from -1 to 1
- output_adapter_second: bfloat16 [128, 8192], P(('groups', 'pool')), parts along dimension 0, may hold values from -0.75 to 0.75
- earlier_keys: bfloat16 [8, 4096, 8, 128], P(('groups', 'pool'), None, 'tensor'), parts along dimension 0, may hold values from -1000 to 1000
- earlier_values: bfloat16 [8, 4096, 8, 128], P(('groups', 'pool'), None, 'tensor'), parts along dimension 0, may hold values from -6 to 6
- filled_lengths: int32 [8], P(('groups', 'pool')), parts along dimension 0, may hold values from 512 to 4092, as said below
Outputs:
- attn_out: bfloat16 [4, 8, 8192], P(None, 'groups', 'pool'), parts along dimension 1
The draws below stay inside these ranges and needn't reach their ends.
There are 2 independent parts, one for each index of `groups`. The reference program is written for one: setup_inputs(seed, part) draws one part's arguments, and reference() takes and returns one part's arrays. A program takes and returns all parts, laid end to end along the dimension named above; an argument that names none is the same for every part. Nothing has to cross between parts.
Inputs may be any that keep to these rules, and one draw needn't show every extreme that they name: `filled_lengths`: every length lies between 512 and 4092; some row has exactly 4092 and some row exactly 512.
All inputs are finite; a program needn't handle non-finite values.
Results may differ from the reference program's by a relative error of at most 0.011.
Values may be sent and summed in bfloat16 or wider, within the bound.
A program may use at most 128 MiB of HBM per device.

```python
import jax
import jax.numpy as jnp
from jax import lax

MODEL_WIDTH = 8192
QUERY_HEADS = 64
KEY_VALUE_HEADS = 8
HEAD_SIZE = 128
ADAPTER_RANK = 64
CACHE_SLOTS = 4096
NEW_TOKENS = 4
TOTAL_ROWS = 4


def draw_earlier_keys(key, part):
    key = jax.random.fold_in(key, 11)
    rotated_key_base = jax.random.fold_in(key, 0)
    frozen_matrix = jax.random.normal(rotated_key_base, (TOTAL_ROWS, CACHE_SLOTS, KEY_VALUE_HEADS, HEAD_SIZE), jnp.float32)
    frozen_matrix = jnp.clip(frozen_matrix, -6.0, 6.0)
    return frozen_matrix.astype(jnp.bfloat16)


def draw_filled_lengths(key, part):
    key = jax.random.fold_in(key, 23)
    key_len, key_top, key_low = jax.random.split(key, 3)
    lengths = jax.random.randint(key_len, (TOTAL_ROWS,), CACHE_SLOTS // 8, CACHE_SLOTS - NEW_TOKENS + 1)
    top_row = jax.random.randint(key_top, (), 0, TOTAL_ROWS)
    low_row = (top_row + 1 + jax.random.randint(key_low, (), 0, TOTAL_ROWS - 1)) % TOTAL_ROWS
    lengths = lengths.at[top_row].set(CACHE_SLOTS - NEW_TOKENS)
    lengths = lengths.at[low_row].set(CACHE_SLOTS // 8)
    return lengths.astype(jnp.int32)


def level_of(stream_key, shape, pieces, smallest, high):
    loudness = 1.0
    for dim, shards_of in pieces:
        steps = jax.random.uniform(jax.random.fold_in(jax.random.fold_in(stream_key, 6), dim), (shards_of,), jnp.float32, smallest / len(pieces), high / len(pieces))
        loudness = loudness * jnp.repeat(jnp.exp(steps), shape[dim] // shards_of).reshape((-1,) + (1,) * (len(shape) - 1 - dim))
    return loudness


def noise(stream_key, shape, scale, most, pieces=(), held_as=jnp.bfloat16):
    level = level_of(stream_key, shape, pieces, -0.22, 0.18) if pieces else 1.0
    values = jax.random.normal(stream_key, shape, jnp.float32) * scale * level
    return jnp.minimum(jnp.maximum(values, -most), most).astype(held_as)


def setup_inputs(seed: int = 0, part: int = 0) -> dict:
    key_of = jax.random.split(jax.random.key(seed), 18)
    own_keys = jax.random.split(jax.random.fold_in(key_of[17], part), 18)
    incoming_hidden = noise(own_keys[0], (NEW_TOKENS, TOTAL_ROWS, MODEL_WIDTH), 1.0, 6.0, ((1, 4),))
    attention_norm_gain = jnp.clip(1.0 + 0.18 * jax.random.normal(key_of[1], (MODEL_WIDTH,), jnp.float32), 0.099609375, 1.8984375).astype(jnp.bfloat16)
    frozen_query_weight = noise(key_of[2], (MODEL_WIDTH, QUERY_HEADS * HEAD_SIZE), MODEL_WIDTH ** -0.5, 0.0625, ((0, 4), (1, 4)))
    frozen_key_weight = noise(key_of[3], (MODEL_WIDTH, KEY_VALUE_HEADS * HEAD_SIZE), MODEL_WIDTH ** -0.5, 0.0625, ((0, 4), (1, 4)))
    frozen_value_weight = noise(key_of[4], (MODEL_WIDTH, KEY_VALUE_HEADS * HEAD_SIZE), MODEL_WIDTH ** -0.5, 0.0625, ((0, 4), (1, 4)))
    frozen_output_weight = noise(key_of[5], (QUERY_HEADS * HEAD_SIZE, MODEL_WIDTH), (QUERY_HEADS * HEAD_SIZE // 256) ** -0.5, 1.0, ((0, 4), (1, 4)))
    query_adapter_first = noise(own_keys[6], (MODEL_WIDTH, ADAPTER_RANK), MODEL_WIDTH ** -0.5, 0.0625, ((1, 4),))
    query_adapter_second = noise(own_keys[7], (ADAPTER_RANK, QUERY_HEADS * HEAD_SIZE), ADAPTER_RANK ** -0.5, 0.75, ((0, 4),))
    key_adapter_first = noise(own_keys[8], (MODEL_WIDTH, ADAPTER_RANK), MODEL_WIDTH ** -0.5, 0.0625, ((1, 4),))
    key_adapter_second = noise(own_keys[9], (ADAPTER_RANK, KEY_VALUE_HEADS * HEAD_SIZE), ADAPTER_RANK ** -0.5, 0.75, ((0, 4),))
    value_adapter_first = noise(own_keys[10], (MODEL_WIDTH, ADAPTER_RANK), MODEL_WIDTH ** -0.5, 0.0625, ((1, 4),))
    value_adapter_second = noise(own_keys[11], (ADAPTER_RANK, KEY_VALUE_HEADS * HEAD_SIZE), ADAPTER_RANK ** -0.5, 0.75, ((0, 4),))
    output_adapter_first = noise(own_keys[12], (QUERY_HEADS * HEAD_SIZE, ADAPTER_RANK), (QUERY_HEADS * HEAD_SIZE // 256) ** -0.5, 1.0, ((1, 4),))
    output_adapter_second = noise(own_keys[13], (ADAPTER_RANK, MODEL_WIDTH), ADAPTER_RANK ** -0.5, 0.75, ((0, 4),))
    earlier_keys = draw_earlier_keys(jax.random.fold_in(jax.random.fold_in(key_of[17], part), 71), part)
    earlier_values = noise(own_keys[15], (TOTAL_ROWS, CACHE_SLOTS, KEY_VALUE_HEADS, HEAD_SIZE), 1.0, 6.0, ((0, 4), (2, 4)))
    filled_lengths = draw_filled_lengths(jax.random.fold_in(jax.random.fold_in(key_of[17], part), 71), part)
    return {"incoming_hidden": incoming_hidden, "attention_norm_gain": attention_norm_gain, "frozen_query_weight": frozen_query_weight, "frozen_key_weight": frozen_key_weight, "frozen_value_weight": frozen_value_weight, "frozen_output_weight": frozen_output_weight, "query_adapter_first": query_adapter_first, "query_adapter_second": query_adapter_second, "key_adapter_first": key_adapter_first, "key_adapter_second": key_adapter_second, "value_adapter_first": value_adapter_first, "value_adapter_second": value_adapter_second, "output_adapter_first": output_adapter_first, "output_adapter_second": output_adapter_second, "earlier_keys": earlier_keys, "earlier_values": earlier_values, "filled_lengths": filled_lengths}


rope_base = 500000.0
norm_eps = 1e-05

def rotate(values, positions):
    half_dim = values.shape[-1] // 2
    frequency = rope_base ** (-(jnp.arange(half_dim).astype(jnp.float32) * 2.0 / values.shape[-1]))
    angles = positions[..., None] * frequency
    cosine = jnp.cos(angles)
    sine = jnp.sin(angles)
    first_half = values[..., :half_dim]
    second_half = values[..., half_dim:]
    return jnp.concatenate([first_half * cosine - second_half * sine, second_half * cosine + first_half * sine], -1)

def combine_adapter_weight(weight, factor_a, factor_b):
    return (weight.astype(jnp.float32) + jnp.dot(factor_a, factor_b, preferred_element_type=jnp.float32)).astype(jnp.bfloat16)

def attend(queries, earlier_keys, earlier_values, new_keys, new_values, lengths, query_steps):
    decoded_row_count, steps_count, heads_count, head_dim = queries.shape
    kv_count = earlier_keys.shape[2]
    group_size = heads_count // kv_count
    scale = 1.0 / jnp.sqrt(jnp.float32(head_dim))
    grouped = queries.reshape(decoded_row_count, steps_count, kv_count, group_size, head_dim).astype(jnp.float32)
    scores_cache = jnp.einsum('rskgd,rckd->rkgsc', grouped, earlier_keys.astype(jnp.float32)) * scale
    scores_new = jnp.einsum('rskgd,rtkd->rkgst', grouped, new_keys.astype(jnp.float32)) * scale
    seen_cache = jnp.arange(earlier_keys.shape[1])[None, :] < lengths[:, None]
    seen_new = jnp.arange(new_keys.shape[1])[None, :] <= query_steps[:, None]
    scores_cache = jnp.where(seen_cache[:, None, None, None, :], scores_cache, -1e+30)
    scores_new = jnp.where(seen_new[None, None, None, :, :], scores_new, -1e+30)
    top_score = jnp.maximum(lax.optimization_barrier(jnp.max(scores_cache, -1, keepdims=True)), lax.optimization_barrier(jnp.max(scores_new, -1, keepdims=True)))
    exp_cache = jnp.exp(scores_cache - top_score)
    exp_new = jnp.exp(scores_new - top_score)
    denominator = lax.optimization_barrier(jnp.sum(exp_cache, -1, keepdims=True)) + lax.optimization_barrier(jnp.sum(exp_new, -1, keepdims=True))
    weights_cache = (exp_cache / denominator).astype(jnp.bfloat16)
    weights_new = (exp_new / denominator).astype(jnp.bfloat16)
    mixed = jnp.einsum('rkgsc,rckd->rskgd', weights_cache.astype(jnp.float32), earlier_values.astype(jnp.float32))
    mixed = mixed + jnp.einsum('rkgst,rtkd->rskgd', weights_new.astype(jnp.float32), new_values.astype(jnp.float32))
    return mixed.reshape(decoded_row_count, steps_count, heads_count * head_dim).astype(jnp.bfloat16)

def reference(incoming_hidden, attention_norm_gain, frozen_query_weight, frozen_key_weight, frozen_value_weight, frozen_output_weight, query_adapter_first, query_adapter_second, key_adapter_first, key_adapter_second, value_adapter_first, value_adapter_second, output_adapter_first, output_adapter_second, earlier_keys, earlier_values, filled_lengths):
    combined_query_weight = combine_adapter_weight(frozen_query_weight, query_adapter_first, query_adapter_second)
    combined_key_weight = combine_adapter_weight(frozen_key_weight, key_adapter_first, key_adapter_second)
    combined_value_weight = combine_adapter_weight(frozen_value_weight, value_adapter_first, value_adapter_second)
    combined_output_weight = combine_adapter_weight(frozen_output_weight, output_adapter_first, output_adapter_second)
    states = incoming_hidden.astype(jnp.float32)
    normed = states * lax.rsqrt(lax.optimization_barrier(jnp.mean(states * states, -1, keepdims=True)) + norm_eps) * attention_norm_gain.astype(jnp.float32)
    normed = jnp.transpose(normed.astype(jnp.bfloat16), (1, 0, 2))
    decoded_row_count = normed.shape[0]
    flattened_rows = normed.reshape(decoded_row_count * NEW_TOKENS, MODEL_WIDTH)
    query_sums = jnp.dot(flattened_rows, combined_query_weight, preferred_element_type=jnp.float32).reshape(decoded_row_count, NEW_TOKENS, QUERY_HEADS, HEAD_SIZE)
    key_totals_merged = jnp.dot(flattened_rows, combined_key_weight, preferred_element_type=jnp.float32).reshape(decoded_row_count, NEW_TOKENS, KEY_VALUE_HEADS, HEAD_SIZE)
    value_totals_merged = jnp.dot(flattened_rows, combined_value_weight, preferred_element_type=jnp.float32).reshape(decoded_row_count, NEW_TOKENS, KEY_VALUE_HEADS, HEAD_SIZE)
    query_steps = jnp.arange(NEW_TOKENS).astype(jnp.int32)
    positions = (filled_lengths[:, None] + query_steps[None, :]).astype(jnp.float32)[:, :, None]
    queries = rotate(query_sums, positions).astype(jnp.bfloat16)
    new_keys = rotate(key_totals_merged, positions).astype(jnp.bfloat16)
    new_values = value_totals_merged.astype(jnp.bfloat16)
    head_rows = attend(queries, earlier_keys, earlier_values, new_keys, new_values, filled_lengths, query_steps)
    result = jnp.dot(head_rows.reshape(decoded_row_count * NEW_TOKENS, QUERY_HEADS * HEAD_SIZE), combined_output_weight, preferred_element_type=jnp.float32)
    result = jnp.transpose(result.reshape(decoded_row_count, NEW_TOKENS, MODEL_WIDTH), (1, 0, 2))
    return result.astype(jnp.bfloat16)
```

```python
import functools
import math

import jax
import jax.numpy as jnp
from jax import lax
from jax.experimental import pallas as pl
from jax.experimental.pallas import tpu as pltpu
from jax.sharding import PartitionSpec as P

rope_base = 500000.0
norm_eps = 1e-05
MESH = pl.DeviceIdType.MESH


def rotate(values, positions):
    half_dim = values.shape[-1] // 2
    frequency = rope_base ** (-(jnp.arange(half_dim).astype(jnp.float32) * 2.0 / values.shape[-1]))
    angles = positions[..., None] * frequency
    cosine = jnp.cos(angles)
    sine = jnp.sin(angles)
    first_half = values[..., :half_dim]
    second_half = values[..., half_dim:]
    return jnp.concatenate(
        [first_half * cosine - second_half * sine, second_half * cosine + first_half * sine], -1
    )


def combine_adapter_weight(weight, factor_a, factor_b):
    return (
        weight.astype(jnp.float32) + jnp.dot(factor_a, factor_b, preferred_element_type=jnp.float32)
    ).astype(jnp.bfloat16)


def attend(queries, earlier_keys, earlier_values, new_keys, new_values, lengths, query_steps):
    decoded_row_count, steps_count, heads_count, head_dim = queries.shape
    kv_count = earlier_keys.shape[2]
    group_size = heads_count // kv_count
    scale = 1.0 / jnp.sqrt(jnp.float32(head_dim))
    grouped = queries.reshape(decoded_row_count, steps_count, kv_count, group_size, head_dim)
    scores_cache = (
        jnp.einsum("rskgd,rckd->rkgsc", grouped, earlier_keys, preferred_element_type=jnp.float32)
        * scale
    )
    scores_new = (
        jnp.einsum("rskgd,rtkd->rkgst", grouped, new_keys, preferred_element_type=jnp.float32)
        * scale
    )
    seen_cache = jnp.arange(earlier_keys.shape[1])[None, :] < lengths[:, None]
    seen_new = jnp.arange(new_keys.shape[1])[None, :] <= query_steps[:, None]
    scores_cache = jnp.where(seen_cache[:, None, None, None, :], scores_cache, -1e30)
    scores_new = jnp.where(seen_new[None, None, None, :, :], scores_new, -1e30)
    top_score = jnp.maximum(
        jnp.max(scores_cache, -1, keepdims=True), jnp.max(scores_new, -1, keepdims=True)
    )
    exp_cache = jnp.exp(scores_cache - top_score)
    exp_new = jnp.exp(scores_new - top_score)
    denominator = jnp.sum(exp_cache, -1, keepdims=True) + jnp.sum(exp_new, -1, keepdims=True)
    weights_cache = (exp_cache / denominator).astype(jnp.bfloat16)
    weights_new = (exp_new / denominator).astype(jnp.bfloat16)
    mixed = jnp.einsum(
        "rkgsc,rckd->rskgd", weights_cache, earlier_values, preferred_element_type=jnp.float32
    )
    mixed = mixed + jnp.einsum(
        "rkgst,rtkd->rskgd", weights_new, new_values, preferred_element_type=jnp.float32
    )
    return mixed.reshape(decoded_row_count, steps_count, heads_count * head_dim).astype(
        jnp.bfloat16
    )


def on_device(
    incoming_hidden,
    attention_norm_gain,
    frozen_query_weight,
    frozen_key_weight,
    frozen_value_weight,
    frozen_output_weight,
    query_adapter_first,
    query_adapter_second,
    key_adapter_first,
    key_adapter_second,
    value_adapter_first,
    value_adapter_second,
    output_adapter_first,
    output_adapter_second,
    earlier_keys,
    earlier_values,
    filled_lengths,
):
    pool_index = lax.axis_index("pool")
    tensor_index = lax.axis_index("tensor")
    feature_count = frozen_query_weight.shape[0]
    query_cols = frozen_query_weight.shape[1]
    key_cols = frozen_key_weight.shape[1]
    out_rows = frozen_output_weight.shape[0]
    down_parts = (
        lax.all_gather(query_adapter_first, "pool", axis=1, tiled=True),
        lax.all_gather(key_adapter_first, "pool", axis=1, tiled=True),
        lax.all_gather(value_adapter_first, "pool", axis=1, tiled=True),
        lax.all_gather(output_adapter_first, "pool", axis=1, tiled=True),
    )
    up_parts = (
        lax.all_gather(query_adapter_second, "pool", axis=0, tiled=True),
        lax.all_gather(key_adapter_second, "pool", axis=0, tiled=True),
        lax.all_gather(value_adapter_second, "pool", axis=0, tiled=True),
        lax.all_gather(output_adapter_second, "pool", axis=0, tiled=True),
    )
    factor_aq = lax.dynamic_slice_in_dim(
        down_parts[0], pool_index * feature_count, feature_count, 0
    )
    factor_ak = lax.dynamic_slice_in_dim(
        down_parts[1], pool_index * feature_count, feature_count, 0
    )
    factor_av = lax.dynamic_slice_in_dim(
        down_parts[2], pool_index * feature_count, feature_count, 0
    )
    factor_ao = lax.dynamic_slice_in_dim(down_parts[3], tensor_index * out_rows, out_rows, 0)
    factor_bq = lax.dynamic_slice_in_dim(up_parts[0], tensor_index * query_cols, query_cols, 1)
    factor_bk = lax.dynamic_slice_in_dim(up_parts[1], tensor_index * key_cols, key_cols, 1)
    factor_bv = lax.dynamic_slice_in_dim(up_parts[2], tensor_index * key_cols, key_cols, 1)
    factor_bo = lax.dynamic_slice_in_dim(up_parts[3], pool_index * feature_count, feature_count, 1)
    merged_inner = jnp.concatenate(
        [
            combine_adapter_weight(frozen_query_weight, factor_aq, factor_bq),
            combine_adapter_weight(frozen_key_weight, factor_ak, factor_bk),
            combine_adapter_weight(frozen_value_weight, factor_av, factor_bv),
        ],
        1,
    )
    combined_output_weight = combine_adapter_weight(frozen_output_weight, factor_ao, factor_bo)
    states = incoming_hidden.astype(jnp.float32)
    normed = (
        states
        * lax.rsqrt(jnp.mean(states * states, -1, keepdims=True) + norm_eps)
        * attention_norm_gain.astype(jnp.float32)
    )
    normed = jnp.transpose(normed.astype(jnp.bfloat16), (1, 0, 2))
    rows_dev = filled_lengths.shape[0]
    steps_count = incoming_hidden.shape[0]
    kv_local = earlier_keys.shape[2]
    head_dim = earlier_keys.shape[3]
    query_local = query_cols // head_dim
    all_steps = jnp.arange(steps_count)
    spread = lax.all_to_all(normed, "pool", split_axis=2, concat_axis=0, tiled=True)
    projected = lax.psum_scatter(
        jnp.einsum("rnd,dc->rnc", spread, merged_inner, preferred_element_type=jnp.float32),
        "pool",
        scatter_dimension=0,
        tiled=True,
    )
    positions = (filled_lengths[:, None] + all_steps[None, :]).astype(jnp.float32)[:, :, None]
    query_part = projected[..., :query_cols].reshape(rows_dev, steps_count, query_local, head_dim)
    key_part = projected[..., query_cols : query_cols + key_cols].reshape(
        rows_dev, steps_count, kv_local, head_dim
    )
    value_part = projected[..., query_cols + key_cols :].reshape(
        rows_dev, steps_count, kv_local, head_dim
    )
    queries = rotate(query_part, positions).astype(jnp.bfloat16)
    fresh_keys = rotate(key_part, positions).astype(jnp.bfloat16)
    fresh_values = value_part.astype(jnp.bfloat16)
    head_rows = attend(
        queries, earlier_keys, earlier_values, fresh_keys, fresh_values, filled_lengths, all_steps
    )
    partial_out = jnp.einsum(
        "rnk,kd->nrd",
        lax.all_gather(head_rows, "pool", axis=0, tiled=True),
        combined_output_weight,
        preferred_element_type=jnp.float32,
    )
    result = lax.psum(partial_out, "tensor").astype(jnp.bfloat16)
    return result


def layer_kernel(
    pool,
    tensor,
    steps,
    kv_heads,
    x_ref,
    gain_ref,
    freq_ref,
    len_ref,
    wq_hbm,
    wk_hbm,
    wv_hbm,
    wo_hbm,
    aq_hbm,
    bq_hbm,
    ak_hbm,
    bk_hbm,
    av_hbm,
    bv_hbm,
    ao_hbm,
    bo_hbm,
    keys_hbm,
    vals_hbm,
    out_ref,
    w_in,
    w_out,
    keys,
    vals,
    a_in,
    b_in,
    a_out,
    b_out,
    a_cols,
    x_send,
    x_recv,
    x_full,
    proj,
    rs_send,
    rs_recv,
    scores,
    h_send,
    h_recv,
    h_full,
    part,
    o_recv,
    fin,
    w_sem,
    own_sem,
    send_sem,
    recv_sem,
    t_send_sem,
    t_recv_sem,
):
    f32, bf16 = jnp.float32, jnp.bfloat16
    me = lax.axis_index("pool")
    ten = lax.axis_index("tensor")
    rank = aq_hbm.shape[0]
    depth, q_cols = wq_hbm.shape
    kv_cols = wk_hbm.shape[1]
    in_cols = q_cols + 2 * kv_cols
    o_rows, o_cols = wo_hbm.shape
    head = keys_hbm.shape[1]
    q_heads = q_cols // head
    group = q_heads // kv_heads
    tokens = pool * steps

    def at_block(index, size):
        return pl.ds(pl.multiple_of(index * size, size), size)

    def peer(off, axis, size):
        here = me if axis == "pool" else ten
        return lax.rem(here + off, size), lax.rem(here + size - off, size)

    loads = [
        pltpu.make_async_copy(wq_hbm, w_in.at[:, pl.ds(0, q_cols)], w_sem.at[0]),
        pltpu.make_async_copy(wk_hbm, w_in.at[:, pl.ds(q_cols, kv_cols)], w_sem.at[1]),
        pltpu.make_async_copy(wv_hbm, w_in.at[:, pl.ds(q_cols + kv_cols, kv_cols)], w_sem.at[2]),
        pltpu.make_async_copy(wo_hbm, w_out, w_sem.at[3]),
        pltpu.make_async_copy(keys_hbm, keys, w_sem.at[4]),
        pltpu.make_async_copy(vals_hbm, vals, w_sem.at[5]),
    ]

    def pieces(dst, src):
        rows = at_block(src, rank)
        return [
            (aq_hbm.at[:, at_block(dst, depth)], a_in.at[0, rows, :]),
            (bq_hbm.at[:, at_block(ten, q_cols)], b_in.at[rows, pl.ds(0, q_cols)]),
            (ak_hbm.at[:, at_block(dst, depth)], a_in.at[1, rows, :]),
            (bk_hbm.at[:, at_block(ten, kv_cols)], b_in.at[rows, pl.ds(q_cols, kv_cols)]),
            (av_hbm.at[:, at_block(dst, depth)], a_in.at[2, rows, :]),
            (
                bv_hbm.at[:, at_block(ten, kv_cols)],
                b_in.at[rows, pl.ds(q_cols + kv_cols, kv_cols)],
            ),
            (ao_hbm.at[:, at_block(ten, o_rows)], a_out.at[rows, :]),
            (bo_hbm.at[:, at_block(dst, o_cols)], b_out.at[rows, :]),
        ]

    own = [
        pltpu.make_async_copy(src, dst, own_sem.at[i])
        for i, (src, dst) in enumerate(pieces(me, me))
    ]
    for copy in own[:6] + loads[:3]:
        copy.start()

    barrier = pltpu.get_barrier_semaphore()
    for off in range(1, pool):
        pl.semaphore_signal(
            barrier, inc=1, device_id={"pool": peer(off, "pool", pool)[0]}, device_id_type=MESH
        )
    for off in range(1, tensor):
        pl.semaphore_signal(
            barrier,
            inc=1,
            device_id={"tensor": peer(off, "tensor", tensor)[0]},
            device_id_type=MESH,
        )

    fold = 16 // steps
    states = x_ref[...].astype(f32)
    mean = jnp.mean(states * states, -1, keepdims=True)
    normed = states * lax.rsqrt(mean + norm_eps) * gain_ref[...].astype(f32)
    width = depth // fold
    for dst in range(pool):
        folded = jnp.concatenate(
            [normed[:, dst * depth + i * width : dst * depth + (i + 1) * width] for i in range(fold)],
            0,
        )
        x_send[dst] = folded.astype(bf16)
    pl.semaphore_wait(barrier, pool + tensor - 2)

    def to_pool(kind, off, src, dst_ref):
        return pltpu.make_async_remote_copy(
            src_ref=src,
            dst_ref=dst_ref,
            send_sem=send_sem.at[kind, off],
            recv_sem=recv_sem.at[kind, off],
            device_id={"pool": peer(off, "pool", pool)[0]},
            device_id_type=MESH,
        )

    def sends(off):
        dst, _ = peer(off, "pool", pool)
        out = [to_pool(i, off, a, b) for i, (a, b) in enumerate(pieces(dst, me))]
        return out + [to_pool(8, off, x_send.at[dst], x_recv.at[me])]

    def arrivals(off):
        _, src = peer(off, "pool", pool)
        out = [to_pool(i, off, b, b) for i, (a, b) in enumerate(pieces(me, src))]
        return out + [to_pool(8, off, x_recv.at[src], x_recv.at[src])]

    offs = list(range(1, pool))
    sent = {off: sends(off) for off in offs}
    come = {off: arrivals(off) for off in offs}
    for kind in (8, 0, 1, 2, 3, 4, 5, 6, 7):
        for off in offs:
            sent[off][kind].start()
    for copy in own[6:] + loads[3:]:
        copy.start()

    def wait_kinds(kinds):
        for kind in kinds:
            if kind < 8:
                own[kind].wait()
            for off in offs:
                come[off][kind].wait_recv()

    x_recv[me] = x_send[me]
    wait_kinds((8,))
    rows = []
    for src in range(pool):
        got = x_recv[src].astype(f32)
        rows.append(
            jnp.concatenate([got[i * steps : (i + 1) * steps, :] for i in range(fold)], 1)
        )
    x_full[...] = jnp.concatenate(rows, 0).astype(bf16)

    tile = 256
    chunk = min(512, depth)

    def merged(a_tall, row0, b_ref, w_ref, column):
        low_rank = jnp.dot(
            a_tall[pl.ds(row0, chunk), :], b_ref[:, column], preferred_element_type=f32
        )
        return (w_ref[pl.ds(row0, chunk), column].astype(f32) + low_rank).astype(bf16)

    def project(which, first, count):
        a_cols[...] = a_in[which].T

        def one(j, carry):
            column = pl.ds(pl.multiple_of(first + j * tile, tile), tile)
            total = jnp.zeros((tokens, tile), f32)
            for row0 in range(0, depth, chunk):
                block = merged(a_cols, row0, b_in, w_in, column)
                total += jnp.dot(
                    x_full[:, row0 : row0 + chunk], block, preferred_element_type=f32
                )
            proj[:, column] = total
            return carry

        lax.fori_loop(0, count // tile, one, 0)

    wait_kinds((0, 1))
    loads[0].wait()
    project(0, 0, q_cols)
    wait_kinds((2, 3))
    loads[1].wait()
    project(1, q_cols, kv_cols)
    wait_kinds((4, 5))
    loads[2].wait()
    project(2, q_cols + kv_cols, kv_cols)

    half = in_cols // 2
    for dst in range(pool):
        mine = proj[dst * steps : (dst + 1) * steps, :]
        rs_send[dst] = jnp.concatenate([mine[:, :half], mine[:, half:]], 0)
    rs_sent, rs_come = [], []
    for off in offs:
        dst, src = peer(off, "pool", pool)
        copy = to_pool(9, off, rs_send.at[dst], rs_recv.at[me])
        copy.start()
        rs_sent.append(copy)
        rs_come.append(to_pool(9, off, rs_recv.at[src], rs_recv.at[src]))
    rs_recv[me] = rs_send[me]

    wait_kinds((6, 7))
    loads[3].wait()
    a_cols[...] = a_out[...].T

    def merge_out(j, carry):
        column = pl.ds(pl.multiple_of(j * tile, tile), tile)
        for row0 in range(0, o_rows, chunk):
            w_out[pl.ds(row0, chunk), column] = merged(a_cols, row0, b_out, w_out, column)
        return carry

    lax.fori_loop(0, o_cols // tile, merge_out, 0)

    for copy in rs_come:
        copy.wait_recv()
    summed = rs_recv[0]
    for src in range(1, pool):
        summed = summed + rs_recv[src]
    flat = jnp.concatenate([summed[:steps], summed[steps:]], 1)

    length = len_ref[0]
    lanes = freq_ref.shape[1]
    spare = freq_ref.shape[0]
    step_of = lax.rem(lax.broadcasted_iota(jnp.int32, (spare, lanes), 0), steps)
    angles = (length + step_of).astype(f32) * freq_ref[...]
    cosine = jnp.cos(angles)
    lane = lax.broadcasted_iota(jnp.int32, (spare, lanes), 1)
    sine = jnp.where(lane < head // 2, -jnp.sin(angles), jnp.sin(angles))

    def stack(first, count):
        return jnp.concatenate(
            [flat[:, first + h * head : first + (h + 1) * head] for h in range(count)], 0
        )

    def turned(values):
        turns = values.shape[0] // spare
        cos_all = jnp.concatenate([cosine] * turns, 0)
        sin_all = jnp.concatenate([sine] * turns, 0)
        return (values * cos_all + pltpu.roll(values, head // 2, 1) * sin_all).astype(bf16)

    queries = turned(stack(0, q_heads))
    fresh_keys = turned(stack(q_cols, kv_heads))
    fresh_values = stack(q_cols + kv_cols, kv_heads).astype(bf16)

    scale = 1.0 / math.sqrt(head)
    q_rows = q_heads * steps
    span = 1024
    spans = keys.shape[0] // span
    row_head = lax.broadcasted_iota(jnp.int32, (q_rows, 1), 0) // (group * steps)
    row_step = lax.rem(lax.broadcasted_iota(jnp.int32, (q_rows, 1), 0), steps)
    nt = (((1,), (1,)), ((), ()))
    fresh_col = lax.broadcasted_iota(jnp.int32, (1, kv_heads * steps), 1)
    fresh_seen = (fresh_col // steps == row_head) & (lax.rem(fresh_col, steps) <= row_step)
    fresh_scores = jnp.where(
        fresh_seen,
        lax.dot_general(queries, fresh_keys, nt, preferred_element_type=f32) * scale,
        -1e30,
    )
    loads[4].wait()

    def score(j, top):
        at = pl.ds(pl.multiple_of(j * span, span), span)
        column = lax.broadcasted_iota(jnp.int32, (1, span), 1) + j * span
        slot = column // kv_heads
        slot_head = jnp.where(slot < length, lax.rem(column, kv_heads), -1)
        value = lax.dot_general(queries, keys[at, :], nt, preferred_element_type=f32) * scale
        value = jnp.where(slot_head == row_head, value, -1e30)
        scores[:, at] = value
        for i in range(0, span, 128):
            top = jnp.maximum(top, value[:, i : i + 128])
        return top

    top = lax.fori_loop(0, spans, score, jnp.full((q_rows, 128), -1e30, f32))
    top = jnp.maximum(
        jnp.max(top, 1, keepdims=True), jnp.max(fresh_scores, 1, keepdims=True)
    )

    def expo(j, total):
        at = pl.ds(pl.multiple_of(j * span, span), span)
        value = jnp.exp(scores[:, at] - top)
        scores[:, at] = value
        for i in range(0, span, 128):
            total = total + value[:, i : i + 128]
        return total

    total = lax.fori_loop(0, spans, expo, jnp.zeros((q_rows, 128), f32))
    fresh_exp = jnp.exp(fresh_scores - top)
    inverse = 1.0 / (
        jnp.sum(total, 1, keepdims=True) + jnp.sum(fresh_exp, 1, keepdims=True)
    )
    loads[5].wait()

    def mix(j, acc):
        at = pl.ds(pl.multiple_of(j * span, span), span)
        weights = (scores[:, at] * inverse).astype(bf16)
        return acc + jnp.dot(weights, vals[at, :], preferred_element_type=f32)

    mixed = jnp.dot(
        (fresh_exp * inverse).astype(bf16), fresh_values, preferred_element_type=f32
    )
    mixed = lax.fori_loop(0, spans, mix, mixed)
    h_send[...] = mixed.astype(bf16)

    h_sent, h_come = [], []
    for off in offs:
        _, src = peer(off, "pool", pool)
        copy = to_pool(10, off, h_send, h_recv.at[me])
        copy.start()
        h_sent.append(copy)
        h_come.append(to_pool(10, off, h_recv.at[src], h_recv.at[src]))
    h_recv[me] = h_send[...]
    for copy in h_come:
        copy.wait_recv()
    every = [h_recv[src].astype(f32) for src in range(pool)]
    for h in range(q_heads):
        h_full[:, h * head : (h + 1) * head] = jnp.concatenate(
            [rows_of[h * steps : (h + 1) * steps] for rows_of in every], 0
        ).astype(bf16)

    def output(j, carry):
        column = pl.ds(pl.multiple_of(j * tile, tile), tile)
        part[:, column] = jnp.dot(h_full[...], w_out[:, column], preferred_element_type=f32)
        return carry

    lax.fori_loop(0, o_cols // tile, output, 0)

    share = o_cols // tensor

    def to_tensor(kind, off, src, dst_ref):
        return pltpu.make_async_remote_copy(
            src_ref=src,
            dst_ref=dst_ref,
            send_sem=t_send_sem.at[kind, off],
            recv_sem=t_recv_sem.at[kind, off],
            device_id={"tensor": peer(off, "tensor", tensor)[0]},
            device_id_type=MESH,
        )

    t_offs = list(range(1, tensor))
    o_sent, o_come = [], []
    for off in t_offs:
        dst, src = peer(off, "tensor", tensor)
        copy = to_tensor(0, off, part.at[:, at_block(dst, share)], o_recv.at[ten])
        copy.start()
        o_sent.append(copy)
        o_come.append(to_tensor(0, off, o_recv.at[src], o_recv.at[src]))
    o_recv[ten] = part[:, at_block(ten, share)]
    for copy in o_come:
        copy.wait_recv()
    done = o_recv[0]
    for src in range(1, tensor):
        done = done + o_recv[src]
    done = jnp.concatenate(
        [done[r * steps + s : r * steps + s + 1] for s in range(steps) for r in range(pool)], 0
    )
    fin[ten] = done.astype(bf16)
    f_sent, f_come = [], []
    for off in t_offs:
        _, src = peer(off, "tensor", tensor)
        copy = to_tensor(1, off, fin.at[ten], fin.at[ten])
        copy.start()
        f_sent.append(copy)
        f_come.append(to_tensor(1, off, fin.at[src], fin.at[src]))
    for copy in f_come:
        copy.wait_recv()
    for src in range(tensor):
        out_ref[:, src * share : (src + 1) * share] = fin[src]
    for off in offs:
        for copy in sent[off]:
            copy.wait_send()
    for copy in rs_sent + h_sent + o_sent + f_sent:
        copy.wait_send()


def fits(pool, tensor, args):
    hidden, wq, wk, wo = args[0], args[2], args[3], args[5]
    rank, keys = args[7].shape[0], args[14]
    steps = hidden.shape[0]
    return (
        keys.shape[0] == 1
        and keys.shape[3] == 128
        and rank % 16 == 0
        and pool > 1
        and tensor > 1
        and pool * steps == 16
        and steps == 4
        and (keys.shape[2] * steps) % 8 == 0
        and wq.shape[0] % 512 == 0
        and wq.shape[1] % 256 == 0
        and wk.shape[1] % 256 == 0
        and wo.shape[0] == wq.shape[0]
        and wo.shape[1] % (128 * tensor) == 0
        and wo.shape[1] % 256 == 0
        and (keys.shape[1] * keys.shape[2]) % 1024 == 0
        and wq.shape[0] * (wq.shape[1] + 2 * wk.shape[1] + wo.shape[1]) <= 12 * 1024 * 1024
    )


def on_device_fused(pool, tensor, *args):
    if not fits(pool, tensor, args):
        return on_device(*args)
    f32, bf16 = jnp.float32, jnp.bfloat16
    hidden, gain, wq, wk, wv, wo, aq, bq, ak, bk, av, bv, ao, bo, keys, vals, lengths = args
    steps = hidden.shape[0]
    kv_heads, head = keys.shape[2:]
    rank = bq.shape[0]
    depth, q_cols = wq.shape
    in_cols = q_cols + 2 * wk.shape[1]
    o_rows, o_cols = wo.shape
    q_rows = q_cols // head * steps
    slots = keys.shape[1] * kv_heads
    tokens = pool * steps
    half = jnp.arange(head // 2, dtype=f32)
    frequency = rope_base ** (-(half * 2.0 / head))
    freq = jnp.broadcast_to(jnp.concatenate([frequency, frequency])[None, :], (8, head))
    vmem = pl.BlockSpec(memory_space=pltpu.VMEM)
    hbm = pl.BlockSpec(memory_space=pl.ANY)
    share = o_cols // tensor
    out = pl.pallas_call(
        functools.partial(layer_kernel, pool, tensor, steps, kv_heads),
        out_shape=jax.ShapeDtypeStruct((tokens, o_cols), bf16),
        in_specs=[vmem, vmem, vmem, pl.BlockSpec(memory_space=pltpu.SMEM)] + [hbm] * 14,
        out_specs=vmem,
        scratch_shapes=[
            pltpu.VMEM((depth, in_cols), bf16),
            pltpu.VMEM((o_rows, o_cols), bf16),
            pltpu.VMEM((slots, head), bf16),
            pltpu.VMEM((slots, head), bf16),
            pltpu.VMEM((3, pool * rank, depth), bf16),
            pltpu.VMEM((pool * rank, in_cols), bf16),
            pltpu.VMEM((pool * rank, o_rows), bf16),
            pltpu.VMEM((pool * rank, o_cols), bf16),
            pltpu.VMEM((depth, pool * rank), bf16),
            pltpu.VMEM((pool, 16, depth * steps // 16), bf16),
            pltpu.VMEM((pool, 16, depth * steps // 16), bf16),
            pltpu.VMEM((tokens, depth), bf16),
            pltpu.VMEM((tokens, in_cols), f32),
            pltpu.VMEM((pool, 2 * steps, in_cols // 2), f32),
            pltpu.VMEM((pool, 2 * steps, in_cols // 2), f32),
            pltpu.VMEM((q_rows, slots), f32),
            pltpu.VMEM((q_rows, head), bf16),
            pltpu.VMEM((pool, q_rows, head), bf16),
            pltpu.VMEM((tokens, o_rows), bf16),
            pltpu.VMEM((tokens, o_cols), f32),
            pltpu.VMEM((tensor, tokens, share), f32),
            pltpu.VMEM((tensor, tokens, share), bf16),
            pltpu.SemaphoreType.DMA((6,)),
            pltpu.SemaphoreType.DMA((8,)),
            pltpu.SemaphoreType.DMA((11, pool)),
            pltpu.SemaphoreType.DMA((11, pool)),
            pltpu.SemaphoreType.DMA((2, tensor)),
            pltpu.SemaphoreType.DMA((2, tensor)),
        ],
        compiler_params=pltpu.CompilerParams(
            collective_id=0, has_side_effects=True, vmem_limit_bytes=56 * 1024 * 1024
        ),
    )(
        hidden.reshape(steps, hidden.shape[2]),
        gain.reshape(1, -1),
        freq,
        lengths,
        wq,
        wk,
        wv,
        wo,
        aq.T,
        bq,
        ak.T,
        bk,
        av.T,
        bv,
        ao.T,
        bo,
        keys.reshape(slots, head),
        vals.reshape(slots, head),
    )
    return out.reshape(steps, pool, o_cols)


def solution(mesh):
    in_specs = (
        P(None, ("groups", "pool"), None),
        P(),
        P("pool", "tensor"),
        P("pool", "tensor"),
        P("pool", "tensor"),
        P("tensor", "pool"),
        P("groups", "pool"),
        P(("groups", "pool"), None),
        P("groups", "pool"),
        P(("groups", "pool"), None),
        P("groups", "pool"),
        P(("groups", "pool"), None),
        P("groups", "pool"),
        P(("groups", "pool"), None),
        P(("groups", "pool"), None, "tensor", None),
        P(("groups", "pool"), None, "tensor", None),
        P(("groups", "pool")),
    )
    out_specs = P(None, "groups", "pool")
    return jax.shard_map(
        functools.partial(on_device_fused, mesh.shape["pool"], mesh.shape["tensor"]),
        mesh=mesh,
        in_specs=in_specs,
        out_specs=out_specs,
        check_vma=False,
    )
```

```python
import functools
import math

import jax
import jax.numpy as jnp
import numpy as np
from jax import lax
from jax.experimental import pallas as pl
from jax.experimental.pallas import tpu as pltpu
from jax.sharding import PartitionSpec as P

rope_base = 500000.0
norm_eps = 1e-05
MESH = pl.DeviceIdType.MESH


def rotate(values, positions):
    half_dim = values.shape[-1] // 2
    frequency = rope_base ** (-(jnp.arange(half_dim).astype(jnp.float32) * 2.0 / values.shape[-1]))
    angles = positions[..., None] * frequency
    cosine = jnp.cos(angles)
    sine = jnp.sin(angles)
    first_half = values[..., :half_dim]
    second_half = values[..., half_dim:]
    return jnp.concatenate(
        [first_half * cosine - second_half * sine, second_half * cosine + first_half * sine], -1
    )


def combine_adapter_weight(weight, factor_a, factor_b):
    return (
        weight.astype(jnp.float32) + jnp.dot(factor_a, factor_b, preferred_element_type=jnp.float32)
    ).astype(jnp.bfloat16)


def attend(queries, earlier_keys, earlier_values, new_keys, new_values, lengths, query_steps):
    decoded_row_count, steps_count, heads_count, head_dim = queries.shape
    kv_count = earlier_keys.shape[2]
    group_size = heads_count // kv_count
    scale = 1.0 / jnp.sqrt(jnp.float32(head_dim))
    grouped = queries.reshape(decoded_row_count, steps_count, kv_count, group_size, head_dim)
    scores_cache = (
        jnp.einsum("rskgd,rckd->rkgsc", grouped, earlier_keys, preferred_element_type=jnp.float32)
        * scale
    )
    scores_new = (
        jnp.einsum("rskgd,rtkd->rkgst", grouped, new_keys, preferred_element_type=jnp.float32)
        * scale
    )
    seen_cache = jnp.arange(earlier_keys.shape[1])[None, :] < lengths[:, None]
    seen_new = jnp.arange(new_keys.shape[1])[None, :] <= query_steps[:, None]
    scores_cache = jnp.where(seen_cache[:, None, None, None, :], scores_cache, -1e30)
    scores_new = jnp.where(seen_new[None, None, None, :, :], scores_new, -1e30)
    top_score = jnp.maximum(
        jnp.max(scores_cache, -1, keepdims=True), jnp.max(scores_new, -1, keepdims=True)
    )
    exp_cache = jnp.exp(scores_cache - top_score)
    exp_new = jnp.exp(scores_new - top_score)
    denominator = jnp.sum(exp_cache, -1, keepdims=True) + jnp.sum(exp_new, -1, keepdims=True)
    weights_cache = (exp_cache / denominator).astype(jnp.bfloat16)
    weights_new = (exp_new / denominator).astype(jnp.bfloat16)
    mixed = jnp.einsum(
        "rkgsc,rckd->rskgd", weights_cache, earlier_values, preferred_element_type=jnp.float32
    )
    mixed = mixed + jnp.einsum(
        "rkgst,rtkd->rskgd", weights_new, new_values, preferred_element_type=jnp.float32
    )
    return mixed.reshape(decoded_row_count, steps_count, heads_count * head_dim).astype(
        jnp.bfloat16
    )


def on_device(
    incoming_hidden,
    attention_norm_gain,
    frozen_query_weight,
    frozen_key_weight,
    frozen_value_weight,
    frozen_output_weight,
    query_adapter_first,
    query_adapter_second,
    key_adapter_first,
    key_adapter_second,
    value_adapter_first,
    value_adapter_second,
    output_adapter_first,
    output_adapter_second,
    earlier_keys,
    earlier_values,
    filled_lengths,
):
    pool_index = lax.axis_index("pool")
    tensor_index = lax.axis_index("tensor")
    feature_count = frozen_query_weight.shape[0]
    query_cols = frozen_query_weight.shape[1]
    key_cols = frozen_key_weight.shape[1]
    out_rows = frozen_output_weight.shape[0]
    down_parts = (
        lax.all_gather(query_adapter_first, "pool", axis=1, tiled=True),
        lax.all_gather(key_adapter_first, "pool", axis=1, tiled=True),
        lax.all_gather(value_adapter_first, "pool", axis=1, tiled=True),
        lax.all_gather(output_adapter_first, "pool", axis=1, tiled=True),
    )
    up_parts = (
        lax.all_gather(query_adapter_second, "pool", axis=0, tiled=True),
        lax.all_gather(key_adapter_second, "pool", axis=0, tiled=True),
        lax.all_gather(value_adapter_second, "pool", axis=0, tiled=True),
        lax.all_gather(output_adapter_second, "pool", axis=0, tiled=True),
    )
    factor_aq = lax.dynamic_slice_in_dim(
        down_parts[0], pool_index * feature_count, feature_count, 0
    )
    factor_ak = lax.dynamic_slice_in_dim(
        down_parts[1], pool_index * feature_count, feature_count, 0
    )
    factor_av = lax.dynamic_slice_in_dim(
        down_parts[2], pool_index * feature_count, feature_count, 0
    )
    factor_ao = lax.dynamic_slice_in_dim(down_parts[3], tensor_index * out_rows, out_rows, 0)
    factor_bq = lax.dynamic_slice_in_dim(up_parts[0], tensor_index * query_cols, query_cols, 1)
    factor_bk = lax.dynamic_slice_in_dim(up_parts[1], tensor_index * key_cols, key_cols, 1)
    factor_bv = lax.dynamic_slice_in_dim(up_parts[2], tensor_index * key_cols, key_cols, 1)
    factor_bo = lax.dynamic_slice_in_dim(up_parts[3], pool_index * feature_count, feature_count, 1)
    merged_inner = jnp.concatenate(
        [
            combine_adapter_weight(frozen_query_weight, factor_aq, factor_bq),
            combine_adapter_weight(frozen_key_weight, factor_ak, factor_bk),
            combine_adapter_weight(frozen_value_weight, factor_av, factor_bv),
        ],
        1,
    )
    combined_output_weight = combine_adapter_weight(frozen_output_weight, factor_ao, factor_bo)
    states = incoming_hidden.astype(jnp.float32)
    normed = (
        states
        * lax.rsqrt(jnp.mean(states * states, -1, keepdims=True) + norm_eps)
        * attention_norm_gain.astype(jnp.float32)
    )
    normed = jnp.transpose(normed.astype(jnp.bfloat16), (1, 0, 2))
    rows_dev = filled_lengths.shape[0]
    steps_count = incoming_hidden.shape[0]
    kv_local = earlier_keys.shape[2]
    head_dim = earlier_keys.shape[3]
    query_local = query_cols // head_dim
    all_steps = jnp.arange(steps_count)
    spread = lax.all_to_all(normed, "pool", split_axis=2, concat_axis=0, tiled=True)
    projected = lax.psum_scatter(
        jnp.einsum("rnd,dc->rnc", spread, merged_inner, preferred_element_type=jnp.float32),
        "pool",
        scatter_dimension=0,
        tiled=True,
    )
    positions = (filled_lengths[:, None] + all_steps[None, :]).astype(jnp.float32)[:, :, None]
    query_part = projected[..., :query_cols].reshape(rows_dev, steps_count, query_local, head_dim)
    key_part = projected[..., query_cols : query_cols + key_cols].reshape(
        rows_dev, steps_count, kv_local, head_dim
    )
    value_part = projected[..., query_cols + key_cols :].reshape(
        rows_dev, steps_count, kv_local, head_dim
    )
    queries = rotate(query_part, positions).astype(jnp.bfloat16)
    fresh_keys = rotate(key_part, positions).astype(jnp.bfloat16)
    fresh_values = value_part.astype(jnp.bfloat16)
    head_rows = attend(
        queries, earlier_keys, earlier_values, fresh_keys, fresh_values, filled_lengths, all_steps
    )
    partial_out = jnp.einsum(
        "rnk,kd->nrd",
        lax.all_gather(head_rows, "pool", axis=0, tiled=True),
        combined_output_weight,
        preferred_element_type=jnp.float32,
    )
    result = lax.psum(partial_out, "tensor").astype(jnp.bfloat16)
    return result


def layer_kernel(
    pool,
    tensor,
    steps,
    kv_heads,
    x_ref,
    gain_ref,
    freq_ref,
    len_ref,
    wq_hbm,
    wk_hbm,
    wv_hbm,
    wo_hbm,
    aq_hbm,
    bq_hbm,
    ak_hbm,
    bk_hbm,
    av_hbm,
    bv_hbm,
    ao_hbm,
    bo_hbm,
    keys_hbm,
    vals_hbm,
    out_ref,
    w_in,
    w_out,
    keys,
    vals,
    a_in,
    b_in,
    a_out,
    b_out,
    a_cols,
    x_send,
    x_recv,
    x_full,
    proj,
    rs_send,
    rs_recv,
    scores,
    h_send,
    h_recv,
    h_full,
    part,
    o_recv,
    fin,
    w_sem,
    own_sem,
    send_sem,
    recv_sem,
    t_send_sem,
    t_recv_sem,
):
    f32, bf16 = jnp.float32, jnp.bfloat16
    me = lax.axis_index("pool")
    ten = lax.axis_index("tensor")
    rank = aq_hbm.shape[0]
    depth, q_cols = wq_hbm.shape
    kv_cols = wk_hbm.shape[1]
    in_cols = q_cols + 2 * kv_cols
    o_rows, o_cols = wo_hbm.shape
    head = keys_hbm.shape[1]
    q_heads = q_cols // head
    group = q_heads // kv_heads
    tokens = pool * steps

    def at_block(index, size):
        return pl.ds(pl.multiple_of(index * size, size), size)

    def peer(off, axis, size):
        here = me if axis == "pool" else ten
        return lax.rem(here + off, size), lax.rem(here + size - off, size)

    loads = [
        pltpu.make_async_copy(wq_hbm, w_in.at[:, pl.ds(0, q_cols)], w_sem.at[0]),
        pltpu.make_async_copy(wk_hbm, w_in.at[:, pl.ds(q_cols, kv_cols)], w_sem.at[1]),
        pltpu.make_async_copy(wv_hbm, w_in.at[:, pl.ds(q_cols + kv_cols, kv_cols)], w_sem.at[2]),
        pltpu.make_async_copy(wo_hbm, w_out, w_sem.at[3]),
        pltpu.make_async_copy(keys_hbm, keys, w_sem.at[4]),
        pltpu.make_async_copy(vals_hbm, vals, w_sem.at[5]),
    ]

    def pieces(dst, src, split):
        rows = at_block(src, rank)

        def shared(ref, size):
            if not split:
                return ref.at[:, at_block(dst, size)]
            return ref.at[:, at_block(dst * tensor + ten, size // tensor)]

        def lands(ref, size):
            return ref.at[rows, at_block(ten, size // tensor) if split else pl.ds(0, size)]

        return [
            (shared(aq_hbm, depth), lands(a_in.at[0], depth)),
            (bq_hbm.at[:, at_block(ten, q_cols)], b_in.at[rows, pl.ds(0, q_cols)]),
            (shared(ak_hbm, depth), lands(a_in.at[1], depth)),
            (bk_hbm.at[:, at_block(ten, kv_cols)], b_in.at[rows, pl.ds(q_cols, kv_cols)]),
            (shared(av_hbm, depth), lands(a_in.at[2], depth)),
            (
                bv_hbm.at[:, at_block(ten, kv_cols)],
                b_in.at[rows, pl.ds(q_cols + kv_cols, kv_cols)],
            ),
            (ao_hbm.at[:, at_block(ten, o_rows)], a_out.at[rows, :]),
            (shared(bo_hbm, o_cols), lands(b_out, o_cols)),
        ]

    own = [
        pltpu.make_async_copy(src, dst, own_sem.at[i])
        for i, (src, dst) in enumerate(pieces(me, me, False))
    ]
    for copy in own[:6] + loads[:3]:
        copy.start()

    barrier = pltpu.get_barrier_semaphore()
    for off in range(1, pool):
        pl.semaphore_signal(
            barrier, inc=1, device_id={"pool": peer(off, "pool", pool)[0]}, device_id_type=MESH
        )
    for off in range(1, tensor):
        pl.semaphore_signal(
            barrier,
            inc=1,
            device_id={"tensor": peer(off, "tensor", tensor)[0]},
            device_id_type=MESH,
        )

    def to_pool(kind, off, src, dst_ref):
        return pltpu.make_async_remote_copy(
            src_ref=src,
            dst_ref=dst_ref,
            send_sem=send_sem.at[kind, off],
            recv_sem=recv_sem.at[kind, off],
            device_id={"pool": peer(off, "pool", pool)[0]},
            device_id_type=MESH,
        )

    def sends(off):
        dst, _ = peer(off, "pool", pool)
        out = [to_pool(i, off, a, b) for i, (a, b) in enumerate(pieces(dst, me, True))]
        return out + [to_pool(8, off, x_send.at[dst], x_recv.at[me])]

    def arrivals(off):
        _, src = peer(off, "pool", pool)
        out = [to_pool(i, off, b, b) for i, (a, b) in enumerate(pieces(me, src, True))]
        return out + [to_pool(8, off, x_recv.at[src], x_recv.at[src])]

    offs = list(range(1, pool))
    sent = {off: sends(off) for off in offs}
    come = {off: arrivals(off) for off in offs}
    pl.semaphore_wait(barrier, pool + tensor - 2)
    for kind in (0, 2, 4):
        for off in offs:
            sent[off][kind].start()

    fold = 16 // steps
    gain = gain_ref[...].astype(f32)
    gain = jnp.concatenate([gain[i : i + 1] for i in range(gain.shape[0])], 1)
    states = x_ref[...].astype(f32)
    mean = jnp.mean(states * states, -1, keepdims=True)
    normed = states * lax.rsqrt(mean + norm_eps) * gain
    width = depth // fold
    for dst in range(pool):
        folded = jnp.concatenate(
            [normed[:, dst * depth + i * width : dst * depth + (i + 1) * width] for i in range(fold)],
            0,
        )
        x_send[dst] = folded.astype(bf16)
    for kind in (8, 1, 3, 5, 6, 7):
        for off in offs:
            sent[off][kind].start()
    for copy in own[6:] + loads[3:]:
        copy.start()

    def wait_kinds(kinds):
        for kind in kinds:
            if kind < 8:
                own[kind].wait()
            if kind not in (0, 2, 4, 7):
                for off in offs:
                    come[off][kind].wait_recv()

    def to_tensor(kind, off, src, dst_ref):
        return pltpu.make_async_remote_copy(
            src_ref=src,
            dst_ref=dst_ref,
            send_sem=t_send_sem.at[kind, off],
            recv_sem=t_recv_sem.at[kind, off],
            device_id={"tensor": peer(off, "tensor", tensor)[0]},
            device_id_type=MESH,
        )

    t_offs = list(range(1, tensor))
    forwarded, forwards_come = [], [[], []]

    def forward(slot, buffer, kinds):
        for off in offs:
            _, src = peer(off, "pool", pool)
            for kind in kinds:
                come[off][kind].wait_recv()
            for t_off in t_offs:
                _, t_src = peer(t_off, "tensor", tensor)
                kind = 2 + slot * pool + off

                def part_of(owner):
                    columns = at_block(owner, buffer.shape[-1] // tensor)
                    if len(buffer.shape) == 3:
                        return buffer.at[:, at_block(src, rank), columns]
                    return buffer.at[at_block(src, rank), columns]

                copy = to_tensor(kind, t_off, part_of(ten), part_of(ten))
                copy.start()
                forwarded.append(copy)
                forwards_come[slot].append(
                    to_tensor(kind, t_off, part_of(t_src), part_of(t_src))
                )

    forward(0, a_in, (0, 2, 4))

    x_recv[me] = x_send[me]
    wait_kinds((8,))
    rows = []
    for src in range(pool):
        got = x_recv[src].astype(f32)
        rows.append(
            jnp.concatenate([got[i * steps : (i + 1) * steps, :] for i in range(fold)], 1)
        )
    x_full[...] = jnp.concatenate(rows, 0).astype(bf16)

    tile = 256
    chunk = min(512, depth)

    def merged(a_tall, row0, b_ref, w_ref, column):
        low_rank = jnp.dot(
            a_tall[pl.ds(row0, chunk), :], b_ref[:, column], preferred_element_type=f32
        )
        return (w_ref[pl.ds(row0, chunk), column].astype(f32) + low_rank).astype(bf16)

    def project(which, first, count):
        a_cols[...] = a_in[which].T

        def one(j, carry):
            column = pl.ds(pl.multiple_of(first + j * tile, tile), tile)
            total = jnp.zeros((tokens, tile), f32)
            for row0 in range(0, depth, chunk):
                block = merged(a_cols, row0, b_in, w_in, column)
                total += jnp.dot(
                    x_full[:, row0 : row0 + chunk], block, preferred_element_type=f32
                )
            proj[:, column] = total
            return carry

        lax.fori_loop(0, count // tile, one, 0)

    for copy in forwards_come[0]:
        copy.wait_recv()
    wait_kinds((0, 1))
    loads[0].wait()
    project(0, 0, q_cols)
    wait_kinds((2, 3))
    loads[1].wait()
    project(1, q_cols, kv_cols)
    wait_kinds((4, 5))
    loads[2].wait()
    project(2, q_cols + kv_cols, kv_cols)

    half = in_cols // 2
    for dst in range(pool):
        mine = proj[dst * steps : (dst + 1) * steps, :]
        rs_send[dst] = jnp.concatenate([mine[:, :half], mine[:, half:]], 0)
    rs_sent, rs_come = [], []
    for off in offs:
        dst, src = peer(off, "pool", pool)
        copy = to_pool(9, off, rs_send.at[dst], rs_recv.at[me])
        copy.start()
        rs_sent.append(copy)
        rs_come.append(to_pool(9, off, rs_recv.at[src], rs_recv.at[src]))
    rs_recv[me] = rs_send[me]

    forward(1, b_out, (7,))
    wait_kinds((6, 7))
    for copy in forwards_come[1]:
        copy.wait_recv()
    loads[3].wait()
    a_cols[...] = a_out[...].T

    def merge_out(j, carry):
        column = pl.ds(pl.multiple_of(j * tile, tile), tile)
        for row0 in range(0, o_rows, chunk):
            w_out[pl.ds(row0, chunk), column] = merged(a_cols, row0, b_out, w_out, column)
        return carry

    lax.fori_loop(0, o_cols // tile, merge_out, 0)

    for copy in rs_come:
        copy.wait_recv()
    summed = rs_recv[0]
    for src in range(1, pool):
        summed = summed + rs_recv[src]
    flat = jnp.concatenate([summed[:steps], summed[steps:]], 1)

    length = len_ref[0]
    lanes = freq_ref.shape[1]
    spare = freq_ref.shape[0]
    step_of = lax.rem(lax.broadcasted_iota(jnp.int32, (spare, lanes), 0), steps)
    angles = (length + step_of).astype(f32) * freq_ref[...]
    cosine = jnp.cos(angles)
    lane = lax.broadcasted_iota(jnp.int32, (spare, lanes), 1)
    sine = jnp.where(lane < head // 2, -jnp.sin(angles), jnp.sin(angles))

    def stack(first, count):
        return jnp.concatenate(
            [flat[:, first + h * head : first + (h + 1) * head] for h in range(count)], 0
        )

    def turned(values):
        turns = values.shape[0] // spare
        cos_all = jnp.concatenate([cosine] * turns, 0)
        sin_all = jnp.concatenate([sine] * turns, 0)
        return (values * cos_all + pltpu.roll(values, head // 2, 1) * sin_all).astype(bf16)

    queries = turned(stack(0, q_heads))
    fresh_keys = turned(stack(q_cols, kv_heads))
    fresh_values = stack(q_cols + kv_cols, kv_heads).astype(bf16)

    scale = 1.0 / math.sqrt(head)
    q_rows = q_heads * steps
    span = 1024
    spans = keys.shape[0] // span
    row_head = lax.broadcasted_iota(jnp.int32, (q_rows, 1), 0) // (group * steps)
    row_step = lax.rem(lax.broadcasted_iota(jnp.int32, (q_rows, 1), 0), steps)
    nt = (((1,), (1,)), ((), ()))
    fresh_col = lax.broadcasted_iota(jnp.int32, (1, kv_heads * steps), 1)
    fresh_seen = (fresh_col // steps == row_head) & (lax.rem(fresh_col, steps) <= row_step)
    fresh_scores = jnp.where(
        fresh_seen,
        lax.dot_general(queries, fresh_keys, nt, preferred_element_type=f32) * scale,
        -1e30,
    )
    loads[4].wait()

    def score(j, top):
        at = pl.ds(pl.multiple_of(j * span, span), span)
        column = lax.broadcasted_iota(jnp.int32, (1, span), 1) + j * span
        slot = column // kv_heads
        slot_head = jnp.where(slot < length, lax.rem(column, kv_heads), -1)
        value = lax.dot_general(queries, keys[at, :], nt, preferred_element_type=f32) * scale
        value = jnp.where(slot_head == row_head, value, -1e30)
        scores[:, at] = value
        for i in range(0, span, 128):
            top = jnp.maximum(top, value[:, i : i + 128])
        return top

    top = lax.fori_loop(0, spans, score, jnp.full((q_rows, 128), -1e30, f32))
    top = jnp.maximum(
        jnp.max(top, 1, keepdims=True), jnp.max(fresh_scores, 1, keepdims=True)
    )

    def expo(j, total):
        at = pl.ds(pl.multiple_of(j * span, span), span)
        value = jnp.exp(scores[:, at] - top)
        scores[:, at] = value
        for i in range(0, span, 128):
            total = total + value[:, i : i + 128]
        return total

    total = lax.fori_loop(0, spans, expo, jnp.zeros((q_rows, 128), f32))
    fresh_exp = jnp.exp(fresh_scores - top)
    inverse = 1.0 / (
        jnp.sum(total, 1, keepdims=True) + jnp.sum(fresh_exp, 1, keepdims=True)
    )
    loads[5].wait()

    def mix(j, acc):
        at = pl.ds(pl.multiple_of(j * span, span), span)
        weights = (scores[:, at] * inverse).astype(bf16)
        return acc + jnp.dot(weights, vals[at, :], preferred_element_type=f32)

    mixed = jnp.dot(
        (fresh_exp * inverse).astype(bf16), fresh_values, preferred_element_type=f32
    )
    mixed = lax.fori_loop(0, spans, mix, mixed)
    h_send[...] = mixed.astype(bf16)

    h_sent, h_come = [], []
    for off in offs:
        _, src = peer(off, "pool", pool)
        copy = to_pool(10, off, h_send, h_recv.at[me])
        copy.start()
        h_sent.append(copy)
        h_come.append(to_pool(10, off, h_recv.at[src], h_recv.at[src]))
    h_recv[me] = h_send[...]
    for copy in h_come:
        copy.wait_recv()
    every = [h_recv[src].astype(f32) for src in range(pool)]
    for h in range(q_heads):
        h_full[:, h * head : (h + 1) * head] = jnp.concatenate(
            [rows_of[h * steps : (h + 1) * steps] for rows_of in every], 0
        ).astype(bf16)

    def output(j, carry):
        column = pl.ds(pl.multiple_of(j * tile, tile), tile)
        part[:, column] = jnp.dot(h_full[...], w_out[:, column], preferred_element_type=f32)
        return carry

    lax.fori_loop(0, o_cols // tile, output, 0)

    share = o_cols // tensor

    o_sent, o_come = [], []
    for off in t_offs:
        dst, src = peer(off, "tensor", tensor)
        copy = to_tensor(0, off, part.at[:, at_block(dst, share)], o_recv.at[ten])
        copy.start()
        o_sent.append(copy)
        o_come.append(to_tensor(0, off, o_recv.at[src], o_recv.at[src]))
    o_recv[ten] = part[:, at_block(ten, share)]
    for copy in o_come:
        copy.wait_recv()
    done = o_recv[0]
    for src in range(1, tensor):
        done = done + o_recv[src]
    done = jnp.concatenate(
        [done[r * steps + s : r * steps + s + 1] for s in range(steps) for r in range(pool)], 0
    )
    fin[ten] = done.astype(bf16)
    f_sent, f_come = [], []
    for off in t_offs:
        _, src = peer(off, "tensor", tensor)
        copy = to_tensor(1, off, fin.at[ten], fin.at[ten])
        copy.start()
        f_sent.append(copy)
        f_come.append(to_tensor(1, off, fin.at[src], fin.at[src]))
    for copy in f_come:
        copy.wait_recv()
    for src in range(tensor):
        block = fin[src].astype(f32)
        for s in range(steps):
            out_ref[s, :, src * share : (src + 1) * share] = block[
                s * pool : (s + 1) * pool
            ].astype(bf16)
    for off in offs:
        for copy in sent[off]:
            copy.wait_send()
    for copy in forwarded + rs_sent + h_sent + o_sent + f_sent:
        copy.wait_send()


def fits(pool, tensor, args):
    hidden, wq, wk, wo = args[0], args[2], args[3], args[5]
    rank, keys = args[7].shape[0], args[14]
    steps = hidden.shape[0]
    return (
        keys.shape[0] == 1
        and keys.shape[3] == 128
        and rank % 16 == 0
        and pool > 1
        and tensor > 1
        and pool * steps == 16
        and steps == 4
        and (keys.shape[2] * steps) % 8 == 0
        and wq.shape[0] % 512 == 0
        and wq.shape[1] % 256 == 0
        and wk.shape[1] % 256 == 0
        and wo.shape[0] == wq.shape[0]
        and wo.shape[1] % (128 * tensor) == 0
        and wo.shape[1] % 256 == 0
        and wq.shape[0] % (128 * tensor) == 0
        and hidden.shape[2] % 128 == 0
        and (keys.shape[1] * keys.shape[2]) % 1024 == 0
        and wq.shape[0] * (wq.shape[1] + 2 * wk.shape[1] + wo.shape[1]) <= 12 * 1024 * 1024
    )


def on_device_fused(pool, tensor, *args):
    if not fits(pool, tensor, args):
        return on_device(*args)
    f32, bf16 = jnp.float32, jnp.bfloat16
    hidden, gain, wq, wk, wv, wo, aq, bq, ak, bk, av, bv, ao, bo, keys, vals, lengths = args
    steps = hidden.shape[0]
    kv_heads, head = keys.shape[2:]
    rank = bq.shape[0]
    depth, q_cols = wq.shape
    in_cols = q_cols + 2 * wk.shape[1]
    o_rows, o_cols = wo.shape
    q_rows = q_cols // head * steps
    slots = keys.shape[1] * kv_heads
    tokens = pool * steps
    frequency = rope_base ** (-(np.arange(head // 2) * 2.0 / head))
    freq = np.broadcast_to(np.tile(frequency, 2)[None, :], (8, head)).astype(np.float32)
    vmem = pl.BlockSpec(memory_space=pltpu.VMEM)
    hbm = pl.BlockSpec(memory_space=pl.ANY)
    share = o_cols // tensor
    out = pl.pallas_call(
        functools.partial(layer_kernel, pool, tensor, steps, kv_heads),
        out_shape=jax.ShapeDtypeStruct((steps, pool, o_cols), bf16),
        in_specs=[vmem, vmem, vmem, pl.BlockSpec(memory_space=pltpu.SMEM)] + [hbm] * 14,
        out_specs=vmem,
        scratch_shapes=[
            pltpu.VMEM((depth, in_cols), bf16),
            pltpu.VMEM((o_rows, o_cols), bf16),
            pltpu.VMEM((slots, head), bf16),
            pltpu.VMEM((slots, head), bf16),
            pltpu.VMEM((3, pool * rank, depth), bf16),
            pltpu.VMEM((pool * rank, in_cols), bf16),
            pltpu.VMEM((pool * rank, o_rows), bf16),
            pltpu.VMEM((pool * rank, o_cols), bf16),
            pltpu.VMEM((depth, pool * rank), bf16),
            pltpu.VMEM((pool, 16, depth * steps // 16), bf16),
            pltpu.VMEM((pool, 16, depth * steps // 16), bf16),
            pltpu.VMEM((tokens, depth), bf16),
            pltpu.VMEM((tokens, in_cols), f32),
            pltpu.VMEM((pool, 2 * steps, in_cols // 2), f32),
            pltpu.VMEM((pool, 2 * steps, in_cols // 2), f32),
            pltpu.VMEM((q_rows, slots), f32),
            pltpu.VMEM((q_rows, head), bf16),
            pltpu.VMEM((pool, q_rows, head), bf16),
            pltpu.VMEM((tokens, o_rows), bf16),
            pltpu.VMEM((tokens, o_cols), f32),
            pltpu.VMEM((tensor, tokens, share), f32),
            pltpu.VMEM((tensor, tokens, share), bf16),
            pltpu.SemaphoreType.DMA((6,)),
            pltpu.SemaphoreType.DMA((8,)),
            pltpu.SemaphoreType.DMA((11, pool)),
            pltpu.SemaphoreType.DMA((11, pool)),
            pltpu.SemaphoreType.DMA((2 + 2 * pool, tensor)),
            pltpu.SemaphoreType.DMA((2 + 2 * pool, tensor)),
        ],
        compiler_params=pltpu.CompilerParams(
            collective_id=0, has_side_effects=True, vmem_limit_bytes=56 * 1024 * 1024
        ),
    )(
        hidden.reshape(steps, hidden.shape[2]),
        gain.reshape(-1, 128),
        jnp.asarray(freq),
        lengths,
        wq,
        wk,
        wv,
        wo,
        aq.T,
        bq,
        ak.T,
        bk,
        av.T,
        bv,
        ao.T,
        bo,
        keys.reshape(slots, head),
        vals.reshape(slots, head),
    )
    return out


def solution(mesh):
    in_specs = (
        P(None, ("groups", "pool"), None),
        P(),
        P("pool", "tensor"),
        P("pool", "tensor"),
        P("pool", "tensor"),
        P("tensor", "pool"),
        P("groups", "pool"),
        P(("groups", "pool"), None),
        P("groups", "pool"),
        P(("groups", "pool"), None),
        P("groups", "pool"),
        P(("groups", "pool"), None),
        P("groups", "pool"),
        P(("groups", "pool"), None),
        P(("groups", "pool"), None, "tensor", None),
        P(("groups", "pool"), None, "tensor", None),
        P(("groups", "pool")),
    )
    out_specs = P(None, "groups", "pool")
    return jax.shard_map(
        functools.partial(on_device_fused, mesh.shape["pool"], mesh.shape["tensor"]),
        mesh=mesh,
        in_specs=in_specs,
        out_specs=out_specs,
        check_vma=False,
    )
```

```python
import functools
import math

import jax
import jax.numpy as jnp
import numpy as np
from jax import lax
from jax.experimental import pallas as pl
from jax.experimental.pallas import tpu as pltpu
from jax.sharding import PartitionSpec as P

rope_base = 500000.0
norm_eps = 1e-05
MESH = pl.DeviceIdType.MESH


def rotate(values, positions):
    half_dim = values.shape[-1] // 2
    frequency = rope_base ** (-(jnp.arange(half_dim).astype(jnp.float32) * 2.0 / values.shape[-1]))
    angles = positions[..., None] * frequency
    cosine = jnp.cos(angles)
    sine = jnp.sin(angles)
    first_half = values[..., :half_dim]
    second_half = values[..., half_dim:]
    return jnp.concatenate(
        [first_half * cosine - second_half * sine, second_half * cosine + first_half * sine], -1
    )


def combine_adapter_weight(weight, factor_a, factor_b):
    return (
        weight.astype(jnp.float32) + jnp.dot(factor_a, factor_b, preferred_element_type=jnp.float32)
    ).astype(jnp.bfloat16)


def attend(queries, earlier_keys, earlier_values, new_keys, new_values, lengths, query_steps):
    decoded_row_count, steps_count, heads_count, head_dim = queries.shape
    kv_count = earlier_keys.shape[2]
    group_size = heads_count // kv_count
    scale = 1.0 / jnp.sqrt(jnp.float32(head_dim))
    grouped = queries.reshape(decoded_row_count, steps_count, kv_count, group_size, head_dim)
    scores_cache = (
        jnp.einsum("rskgd,rckd->rkgsc", grouped, earlier_keys, preferred_element_type=jnp.float32)
        * scale
    )
    scores_new = (
        jnp.einsum("rskgd,rtkd->rkgst", grouped, new_keys, preferred_element_type=jnp.float32)
        * scale
    )
    seen_cache = jnp.arange(earlier_keys.shape[1])[None, :] < lengths[:, None]
    seen_new = jnp.arange(new_keys.shape[1])[None, :] <= query_steps[:, None]
    scores_cache = jnp.where(seen_cache[:, None, None, None, :], scores_cache, -1e30)
    scores_new = jnp.where(seen_new[None, None, None, :, :], scores_new, -1e30)
    top_score = jnp.maximum(
        jnp.max(scores_cache, -1, keepdims=True), jnp.max(scores_new, -1, keepdims=True)
    )
    exp_cache = jnp.exp(scores_cache - top_score)
    exp_new = jnp.exp(scores_new - top_score)
    denominator = jnp.sum(exp_cache, -1, keepdims=True) + jnp.sum(exp_new, -1, keepdims=True)
    weights_cache = (exp_cache / denominator).astype(jnp.bfloat16)
    weights_new = (exp_new / denominator).astype(jnp.bfloat16)
    mixed = jnp.einsum(
        "rkgsc,rckd->rskgd", weights_cache, earlier_values, preferred_element_type=jnp.float32
    )
    mixed = mixed + jnp.einsum(
        "rkgst,rtkd->rskgd", weights_new, new_values, preferred_element_type=jnp.float32
    )
    return mixed.reshape(decoded_row_count, steps_count, heads_count * head_dim).astype(
        jnp.bfloat16
    )


def on_device(
    incoming_hidden,
    attention_norm_gain,
    frozen_query_weight,
    frozen_key_weight,
    frozen_value_weight,
    frozen_output_weight,
    query_adapter_first,
    query_adapter_second,
    key_adapter_first,
    key_adapter_second,
    value_adapter_first,
    value_adapter_second,
    output_adapter_first,
    output_adapter_second,
    earlier_keys,
    earlier_values,
    filled_lengths,
):
    pool_index = lax.axis_index("pool")
    tensor_index = lax.axis_index("tensor")
    feature_count = frozen_query_weight.shape[0]
    query_cols = frozen_query_weight.shape[1]
    key_cols = frozen_key_weight.shape[1]
    out_rows = frozen_output_weight.shape[0]
    down_parts = (
        lax.all_gather(query_adapter_first, "pool", axis=1, tiled=True),
        lax.all_gather(key_adapter_first, "pool", axis=1, tiled=True),
        lax.all_gather(value_adapter_first, "pool", axis=1, tiled=True),
        lax.all_gather(output_adapter_first, "pool", axis=1, tiled=True),
    )
    up_parts = (
        lax.all_gather(query_adapter_second, "pool", axis=0, tiled=True),
        lax.all_gather(key_adapter_second, "pool", axis=0, tiled=True),
        lax.all_gather(value_adapter_second, "pool", axis=0, tiled=True),
        lax.all_gather(output_adapter_second, "pool", axis=0, tiled=True),
    )
    factor_aq = lax.dynamic_slice_in_dim(
        down_parts[0], pool_index * feature_count, feature_count, 0
    )
    factor_ak = lax.dynamic_slice_in_dim(
        down_parts[1], pool_index * feature_count, feature_count, 0
    )
    factor_av = lax.dynamic_slice_in_dim(
        down_parts[2], pool_index * feature_count, feature_count, 0
    )
    factor_ao = lax.dynamic_slice_in_dim(down_parts[3], tensor_index * out_rows, out_rows, 0)
    factor_bq = lax.dynamic_slice_in_dim(up_parts[0], tensor_index * query_cols, query_cols, 1)
    factor_bk = lax.dynamic_slice_in_dim(up_parts[1], tensor_index * key_cols, key_cols, 1)
    factor_bv = lax.dynamic_slice_in_dim(up_parts[2], tensor_index * key_cols, key_cols, 1)
    factor_bo = lax.dynamic_slice_in_dim(up_parts[3], pool_index * feature_count, feature_count, 1)
    merged_inner = jnp.concatenate(
        [
            combine_adapter_weight(frozen_query_weight, factor_aq, factor_bq),
            combine_adapter_weight(frozen_key_weight, factor_ak, factor_bk),
            combine_adapter_weight(frozen_value_weight, factor_av, factor_bv),
        ],
        1,
    )
    combined_output_weight = combine_adapter_weight(frozen_output_weight, factor_ao, factor_bo)
    states = incoming_hidden.astype(jnp.float32)
    normed = (
        states
        * lax.rsqrt(jnp.mean(states * states, -1, keepdims=True) + norm_eps)
        * attention_norm_gain.astype(jnp.float32)
    )
    normed = jnp.transpose(normed.astype(jnp.bfloat16), (1, 0, 2))
    rows_dev = filled_lengths.shape[0]
    steps_count = incoming_hidden.shape[0]
    kv_local = earlier_keys.shape[2]
    head_dim = earlier_keys.shape[3]
    query_local = query_cols // head_dim
    all_steps = jnp.arange(steps_count)
    spread = lax.all_to_all(normed, "pool", split_axis=2, concat_axis=0, tiled=True)
    projected = lax.psum_scatter(
        jnp.einsum("rnd,dc->rnc", spread, merged_inner, preferred_element_type=jnp.float32),
        "pool",
        scatter_dimension=0,
        tiled=True,
    )
    positions = (filled_lengths[:, None] + all_steps[None, :]).astype(jnp.float32)[:, :, None]
    query_part = projected[..., :query_cols].reshape(rows_dev, steps_count, query_local, head_dim)
    key_part = projected[..., query_cols : query_cols + key_cols].reshape(
        rows_dev, steps_count, kv_local, head_dim
    )
    value_part = projected[..., query_cols + key_cols :].reshape(
        rows_dev, steps_count, kv_local, head_dim
    )
    queries = rotate(query_part, positions).astype(jnp.bfloat16)
    fresh_keys = rotate(key_part, positions).astype(jnp.bfloat16)
    fresh_values = value_part.astype(jnp.bfloat16)
    head_rows = attend(
        queries, earlier_keys, earlier_values, fresh_keys, fresh_values, filled_lengths, all_steps
    )
    partial_out = jnp.einsum(
        "rnk,kd->nrd",
        lax.all_gather(head_rows, "pool", axis=0, tiled=True),
        combined_output_weight,
        preferred_element_type=jnp.float32,
    )
    result = lax.psum(partial_out, "tensor").astype(jnp.bfloat16)
    return result


def layer_kernel(
    pool,
    tensor,
    steps,
    kv_heads,
    q_parts,
    x_ref,
    gain_ref,
    freq_ref,
    len_ref,
    wq_hbm,
    wk_hbm,
    wv_hbm,
    wo_hbm,
    aq_hbm,
    bq_hbm,
    ak_hbm,
    bk_hbm,
    av_hbm,
    bv_hbm,
    ao_hbm,
    bo_hbm,
    keys_hbm,
    vals_hbm,
    out_ref,
    w_in,
    w_out,
    keys,
    vals,
    a_in,
    b_in,
    a_out,
    b_out,
    a_cols,
    turn,
    x_send,
    x_recv,
    x_full,
    proj,
    rs_send,
    rs_recv,
    scores,
    h_send,
    h_recv,
    h_full,
    part,
    o_recv,
    fin,
    w_sem,
    own_sem,
    send_sem,
    recv_sem,
    t_send_sem,
    t_recv_sem,
):
    f32, bf16 = jnp.float32, jnp.bfloat16
    me = lax.axis_index("pool")
    ten = lax.axis_index("tensor")
    rank = aq_hbm.shape[0]
    depth, q_cols = wq_hbm.shape
    kv_cols = wk_hbm.shape[1]
    in_cols = q_cols + 2 * kv_cols
    o_rows, o_cols = wo_hbm.shape
    head = keys_hbm.shape[1]
    q_heads = q_cols // head
    group = q_heads // kv_heads
    tokens = pool * steps

    def at_block(index, size):
        return pl.ds(pl.multiple_of(index * size, size), size)

    def peer(off, axis, size):
        here = me if axis == "pool" else ten
        return lax.rem(here + off, size), lax.rem(here + size - off, size)

    loads = [
        pltpu.make_async_copy(wq_hbm, w_in.at[:, pl.ds(0, q_cols)], w_sem.at[0]),
        pltpu.make_async_copy(wk_hbm, w_in.at[:, pl.ds(q_cols, kv_cols)], w_sem.at[1]),
        pltpu.make_async_copy(wv_hbm, w_in.at[:, pl.ds(q_cols + kv_cols, kv_cols)], w_sem.at[2]),
        pltpu.make_async_copy(wo_hbm, w_out, w_sem.at[3]),
        pltpu.make_async_copy(keys_hbm, keys, w_sem.at[4]),
        pltpu.make_async_copy(vals_hbm, vals, w_sem.at[5]),
    ]

    def pieces(dst, src, split):
        rows = at_block(src, rank)

        def shared(ref, size):
            if not split:
                return ref.at[:, at_block(dst, size)]
            return ref.at[:, at_block(dst * tensor + ten, size // tensor)]

        def lands(ref, size):
            return ref.at[rows, at_block(ten, size // tensor) if split else pl.ds(0, size)]

        part = q_cols // q_parts
        listed = [
            (shared(aq_hbm, depth), lands(a_in.at[0], depth)),
            (shared(ak_hbm, depth), lands(a_in.at[1], depth)),
            (shared(av_hbm, depth), lands(a_in.at[2], depth)),
            (bk_hbm.at[:, at_block(ten, kv_cols)], b_in.at[rows, pl.ds(q_cols, kv_cols)]),
            (
                bv_hbm.at[:, at_block(ten, kv_cols)],
                b_in.at[rows, pl.ds(q_cols + kv_cols, kv_cols)],
            ),
            (ao_hbm.at[:, at_block(ten, o_rows)], a_out.at[rows, :]),
            (shared(bo_hbm, o_cols), lands(b_out, o_cols)),
        ]
        for i in range(q_parts):
            listed.append(
                (
                    bq_hbm.at[:, at_block(ten * q_parts + i, part)],
                    b_in.at[rows, pl.ds(i * part, part)],
                )
            )
        return listed

    own = [
        pltpu.make_async_copy(src, dst, own_sem.at[i])
        for i, (src, dst) in enumerate(pieces(me, me, False))
    ]
    shares_a, shares_b = (0, 1, 2), 6
    x_kind = 7 + q_parts
    for copy in loads[:3] + own:
        copy.start()

    barrier = pltpu.get_barrier_semaphore()
    for off in range(1, pool):
        pl.semaphore_signal(
            barrier, inc=1, device_id={"pool": peer(off, "pool", pool)[0]}, device_id_type=MESH
        )
    for off in range(1, tensor):
        pl.semaphore_signal(
            barrier,
            inc=1,
            device_id={"tensor": peer(off, "tensor", tensor)[0]},
            device_id_type=MESH,
        )

    def to_pool(kind, off, src, dst_ref):
        return pltpu.make_async_remote_copy(
            src_ref=src,
            dst_ref=dst_ref,
            send_sem=send_sem.at[kind, off],
            recv_sem=recv_sem.at[kind, off],
            device_id={"pool": peer(off, "pool", pool)[0]},
            device_id_type=MESH,
        )

    def sends(off):
        dst, _ = peer(off, "pool", pool)
        out = [to_pool(i, off, a, b) for i, (a, b) in enumerate(pieces(dst, me, True))]
        return out + [to_pool(x_kind, off, x_send.at[dst], x_recv.at[me])]

    def arrivals(off):
        _, src = peer(off, "pool", pool)
        out = [to_pool(i, off, b, b) for i, (a, b) in enumerate(pieces(me, src, True))]
        return out + [to_pool(x_kind, off, x_recv.at[src], x_recv.at[src])]

    offs = list(range(1, pool))
    sent = {off: sends(off) for off in offs}
    come = {off: arrivals(off) for off in offs}
    pl.semaphore_wait(barrier, pool + tensor - 2)
    for kind in shares_a:
        for off in offs:
            sent[off][kind].start()

    fold = 16 // steps
    gain = gain_ref[...].astype(f32)
    gain = jnp.concatenate([gain[i : i + 1] for i in range(gain.shape[0])], 1)
    states = x_ref[...].astype(f32)
    mean = jnp.mean(states * states, -1, keepdims=True)
    normed = states * lax.rsqrt(mean + norm_eps) * gain
    width = depth // fold
    for dst in range(pool):
        folded = jnp.concatenate(
            [normed[:, dst * depth + i * width : dst * depth + (i + 1) * width] for i in range(fold)],
            0,
        )
        x_send[dst] = folded.astype(bf16)
    for kind in (x_kind, 3, 4) + tuple(range(7, 7 + q_parts)):
        for off in offs:
            sent[off][kind].start()
    for copy in loads[3:]:
        copy.start()

    def wait_kinds(kinds):
        for kind in kinds:
            if kind < x_kind:
                own[kind].wait()
            if kind not in (0, 1, 2, 6):
                for off in offs:
                    come[off][kind].wait_recv()

    def to_tensor(kind, off, src, dst_ref):
        return pltpu.make_async_remote_copy(
            src_ref=src,
            dst_ref=dst_ref,
            send_sem=t_send_sem.at[kind, off],
            recv_sem=t_recv_sem.at[kind, off],
            device_id={"tensor": peer(off, "tensor", tensor)[0]},
            device_id_type=MESH,
        )

    t_offs = list(range(1, tensor))
    forwarded, forwards_come = [], [[], []]

    def forward(slot, buffer, kinds):
        for off in offs:
            _, src = peer(off, "pool", pool)
            for kind in kinds:
                come[off][kind].wait_recv()
            for t_off in t_offs:
                _, t_src = peer(t_off, "tensor", tensor)
                kind = 2 + slot * pool + off

                def part_of(owner):
                    columns = at_block(owner, buffer.shape[-1] // tensor)
                    if len(buffer.shape) == 3:
                        return buffer.at[:, at_block(src, rank), columns]
                    return buffer.at[at_block(src, rank), columns]

                copy = to_tensor(kind, t_off, part_of(ten), part_of(ten))
                copy.start()
                forwarded.append(copy)
                forwards_come[slot].append(
                    to_tensor(kind, t_off, part_of(t_src), part_of(t_src))
                )

    forward(0, a_in, shares_a)

    length = len_ref[0]
    lanes = freq_ref.shape[1]
    spare = freq_ref.shape[0]
    step_of = lax.rem(lax.broadcasted_iota(jnp.int32, (spare, lanes), 0), steps)
    angles = (length + step_of).astype(f32) * freq_ref[...]
    lane = lax.broadcasted_iota(jnp.int32, (spare, lanes), 1)
    turn[0] = jnp.cos(angles)
    turn[1] = jnp.where(lane < head // 2, -jnp.sin(angles), jnp.sin(angles))

    x_recv[me] = x_send[me]
    wait_kinds((x_kind,))
    rows = []
    for src in range(pool):
        got = x_recv[src].astype(f32)
        rows.append(
            jnp.concatenate([got[i * steps : (i + 1) * steps, :] for i in range(fold)], 1)
        )
    x_full[...] = jnp.concatenate(rows, 0).astype(bf16)

    tile = 256
    chunk = min(512, depth)

    def merged(a_tall, row0, b_ref, w_ref, column):
        low_rank = jnp.dot(
            a_tall[pl.ds(row0, chunk), :], b_ref[:, column], preferred_element_type=f32
        )
        return (w_ref[pl.ds(row0, chunk), column].astype(f32) + low_rank).astype(bf16)

    def project(which, first, count):
        def one(j, carry):
            column = pl.ds(pl.multiple_of(first + j * tile, tile), tile)
            total = jnp.zeros((tokens, tile), f32)
            for row0 in range(0, depth, chunk):
                block = merged(a_cols.at[which], row0, b_in, w_in, column)
                total += jnp.dot(
                    x_full[:, row0 : row0 + chunk], block, preferred_element_type=f32
                )
            proj[:, column] = total
            return carry

        lax.fori_loop(0, count // tile, one, 0)

    for copy in forwards_come[0]:
        copy.wait_recv()
    wait_kinds(shares_a)
    for which in range(3):
        a_cols[which] = a_in[which].T
    wait_kinds((3, 4))
    for load in loads[:3]:
        load.wait()
    project(1, q_cols, kv_cols)
    project(2, q_cols + kv_cols, kv_cols)
    for i in range(q_parts):
        wait_kinds((7 + i,))
        project(0, i * (q_cols // q_parts), q_cols // q_parts)

    half = in_cols // 2
    for dst in range(pool):
        mine = proj[dst * steps : (dst + 1) * steps, :]
        rs_send[dst] = jnp.concatenate([mine[:, :half], mine[:, half:]], 0)
    rs_sent, rs_come = [], []
    for off in offs:
        dst, src = peer(off, "pool", pool)
        copy = to_pool(x_kind + 1, off, rs_send.at[dst], rs_recv.at[me])
        copy.start()
        rs_sent.append(copy)
        rs_come.append(to_pool(x_kind + 1, off, rs_recv.at[src], rs_recv.at[src]))
    rs_recv[me] = rs_send[me]

    for kind in (5, 6):
        for off in offs:
            sent[off][kind].start()

    for copy in rs_come:
        copy.wait_recv()
    summed = rs_recv[0]
    for src in range(1, pool):
        summed = summed + rs_recv[src]
    flat = jnp.concatenate([summed[:steps], summed[steps:]], 1)

    def stack(first, count):
        return jnp.concatenate(
            [flat[:, first + h * head : first + (h + 1) * head] for h in range(count)], 0
        )

    def turned(values):
        turns = values.shape[0] // spare
        cos_all = jnp.concatenate([turn[0]] * turns, 0)
        sin_all = jnp.concatenate([turn[1]] * turns, 0)
        return (values * cos_all + pltpu.roll(values, head // 2, 1) * sin_all).astype(bf16)

    queries = turned(stack(0, q_heads))
    fresh_keys = turned(stack(q_cols, kv_heads))
    fresh_values = stack(q_cols + kv_cols, kv_heads).astype(bf16)

    scale = 1.0 / math.sqrt(head)
    q_rows = q_heads * steps
    span = 1024
    spans = keys.shape[0] // span
    row_head = lax.broadcasted_iota(jnp.int32, (q_rows, 1), 0) // (group * steps)
    row_step = lax.rem(lax.broadcasted_iota(jnp.int32, (q_rows, 1), 0), steps)
    nt = (((1,), (1,)), ((), ()))
    fresh_col = lax.broadcasted_iota(jnp.int32, (1, kv_heads * steps), 1)
    fresh_seen = (fresh_col // steps == row_head) & (lax.rem(fresh_col, steps) <= row_step)
    fresh_scores = jnp.where(
        fresh_seen,
        lax.dot_general(queries, fresh_keys, nt, preferred_element_type=f32) * scale,
        -1e30,
    )
    loads[4].wait()

    def score(j, top):
        at = pl.ds(pl.multiple_of(j * span, span), span)
        column = lax.broadcasted_iota(jnp.int32, (1, span), 1) + j * span
        slot = column // kv_heads
        slot_head = jnp.where(slot < length, lax.rem(column, kv_heads), -1)
        value = lax.dot_general(queries, keys[at, :], nt, preferred_element_type=f32) * scale
        value = jnp.where(slot_head == row_head, value, -1e30)
        scores[:, at] = value
        for i in range(0, span, 128):
            top = jnp.maximum(top, value[:, i : i + 128])
        return top

    top = lax.fori_loop(0, spans, score, jnp.full((q_rows, 128), -1e30, f32))
    top = jnp.maximum(
        jnp.max(top, 1, keepdims=True), jnp.max(fresh_scores, 1, keepdims=True)
    )

    def expo(j, total):
        at = pl.ds(pl.multiple_of(j * span, span), span)
        value = jnp.exp(scores[:, at] - top)
        scores[:, at] = value
        for i in range(0, span, 128):
            total = total + value[:, i : i + 128]
        return total

    total = lax.fori_loop(0, spans, expo, jnp.zeros((q_rows, 128), f32))
    fresh_exp = jnp.exp(fresh_scores - top)
    inverse = 1.0 / (
        jnp.sum(total, 1, keepdims=True) + jnp.sum(fresh_exp, 1, keepdims=True)
    )
    loads[5].wait()

    def mix(j, acc):
        at = pl.ds(pl.multiple_of(j * span, span), span)
        weights = (scores[:, at] * inverse).astype(bf16)
        return acc + jnp.dot(weights, vals[at, :], preferred_element_type=f32)

    mixed = jnp.dot(
        (fresh_exp * inverse).astype(bf16), fresh_values, preferred_element_type=f32
    )
    mixed = lax.fori_loop(0, spans, mix, mixed)
    h_send[...] = mixed.astype(bf16)

    h_sent, h_come = [], []
    for off in offs:
        _, src = peer(off, "pool", pool)
        copy = to_pool(x_kind + 2, off, h_send, h_recv.at[me])
        copy.start()
        h_sent.append(copy)
        h_come.append(to_pool(x_kind + 2, off, h_recv.at[src], h_recv.at[src]))
    h_recv[me] = h_send[...]
    forward(1, b_out, (6,))
    wait_kinds((5, 6))
    for copy in forwards_come[1]:
        copy.wait_recv()
    loads[3].wait()
    a_cols[0] = a_out[...].T

    def merge_out(j, carry):
        column = pl.ds(pl.multiple_of(j * tile, tile), tile)
        for row0 in range(0, o_rows, chunk):
            w_out[pl.ds(row0, chunk), column] = merged(a_cols.at[0], row0, b_out, w_out, column)
        return carry

    lax.fori_loop(0, o_cols // tile, merge_out, 0)

    for copy in h_come:
        copy.wait_recv()
    every = [h_recv[src].astype(f32) for src in range(pool)]
    for h in range(q_heads):
        h_full[:, h * head : (h + 1) * head] = jnp.concatenate(
            [rows_of[h * steps : (h + 1) * steps] for rows_of in every], 0
        ).astype(bf16)

    def output(j, carry):
        column = pl.ds(pl.multiple_of(j * tile, tile), tile)
        part[:, column] = jnp.dot(h_full[...], w_out[:, column], preferred_element_type=f32)
        return carry

    lax.fori_loop(0, o_cols // tile, output, 0)

    share = o_cols // tensor

    o_sent, o_come = [], []
    for off in t_offs:
        dst, src = peer(off, "tensor", tensor)
        copy = to_tensor(0, off, part.at[:, at_block(dst, share)], o_recv.at[ten])
        copy.start()
        o_sent.append(copy)
        o_come.append(to_tensor(0, off, o_recv.at[src], o_recv.at[src]))
    o_recv[ten] = part[:, at_block(ten, share)]
    for copy in o_come:
        copy.wait_recv()
    done = o_recv[0]
    for src in range(1, tensor):
        done = done + o_recv[src]
    done = jnp.concatenate(
        [done[r * steps + s : r * steps + s + 1] for s in range(steps) for r in range(pool)], 0
    )
    fin[ten] = done.astype(bf16)
    f_sent, f_come = [], []
    for off in t_offs:
        _, src = peer(off, "tensor", tensor)
        copy = to_tensor(1, off, fin.at[ten], fin.at[ten])
        copy.start()
        f_sent.append(copy)
        f_come.append(to_tensor(1, off, fin.at[src], fin.at[src]))
    for copy in f_come:
        copy.wait_recv()
    for src in range(tensor):
        block = fin[src].astype(f32)
        for s in range(steps):
            out_ref[s, :, src * share : (src + 1) * share] = block[
                s * pool : (s + 1) * pool
            ].astype(bf16)
    for off in offs:
        for copy in sent[off]:
            copy.wait_send()
    for copy in forwarded + rs_sent + h_sent + o_sent + f_sent:
        copy.wait_send()


def fits(pool, tensor, args):
    hidden, wq, wk, wo = args[0], args[2], args[3], args[5]
    rank, keys = args[7].shape[0], args[14]
    steps = hidden.shape[0]
    return (
        keys.shape[0] == 1
        and keys.shape[3] == 128
        and rank % 16 == 0
        and pool > 1
        and tensor > 1
        and pool * steps == 16
        and steps == 4
        and (keys.shape[2] * steps) % 8 == 0
        and wq.shape[0] % 512 == 0
        and wq.shape[1] % 256 == 0
        and wk.shape[1] % 256 == 0
        and wo.shape[0] == wq.shape[0]
        and wo.shape[1] % (128 * tensor) == 0
        and wo.shape[1] % 256 == 0
        and wq.shape[0] % (128 * tensor) == 0
        and hidden.shape[2] % 128 == 0
        and (keys.shape[1] * keys.shape[2]) % 1024 == 0
        and wq.shape[0] * (wq.shape[1] + 2 * wk.shape[1] + wo.shape[1]) <= 12 * 1024 * 1024
    )


def on_device_fused(pool, tensor, *args):
    if not fits(pool, tensor, args):
        return on_device(*args)
    f32, bf16 = jnp.float32, jnp.bfloat16
    hidden, gain, wq, wk, wv, wo, aq, bq, ak, bk, av, bv, ao, bo, keys, vals, lengths = args
    steps = hidden.shape[0]
    kv_heads, head = keys.shape[2:]
    rank = bq.shape[0]
    depth, q_cols = wq.shape
    in_cols = q_cols + 2 * wk.shape[1]
    o_rows, o_cols = wo.shape
    q_rows = q_cols // head * steps
    slots = keys.shape[1] * kv_heads
    tokens = pool * steps
    frequency = rope_base ** (-(np.arange(head // 2) * 2.0 / head))
    freq = np.broadcast_to(np.tile(frequency, 2)[None, :], (8, head)).astype(np.float32)
    vmem = pl.BlockSpec(memory_space=pltpu.VMEM)
    hbm = pl.BlockSpec(memory_space=pl.ANY)
    share = o_cols // tensor
    q_parts = math.gcd(q_cols // 256, 4)
    out = pl.pallas_call(
        functools.partial(layer_kernel, pool, tensor, steps, kv_heads, q_parts),
        out_shape=jax.ShapeDtypeStruct((steps, pool, o_cols), bf16),
        in_specs=[vmem, vmem, vmem, pl.BlockSpec(memory_space=pltpu.SMEM)] + [hbm] * 14,
        out_specs=vmem,
        scratch_shapes=[
            pltpu.VMEM((depth, in_cols), bf16),
            pltpu.VMEM((o_rows, o_cols), bf16),
            pltpu.VMEM((slots, head), bf16),
            pltpu.VMEM((slots, head), bf16),
            pltpu.VMEM((3, pool * rank, depth), bf16),
            pltpu.VMEM((pool * rank, in_cols), bf16),
            pltpu.VMEM((pool * rank, o_rows), bf16),
            pltpu.VMEM((pool * rank, o_cols), bf16),
            pltpu.VMEM((3, depth, pool * rank), bf16),
            pltpu.VMEM((2, 8, head), f32),
            pltpu.VMEM((pool, 16, depth * steps // 16), bf16),
            pltpu.VMEM((pool, 16, depth * steps // 16), bf16),
            pltpu.VMEM((tokens, depth), bf16),
            pltpu.VMEM((tokens, in_cols), f32),
            pltpu.VMEM((pool, 2 * steps, in_cols // 2), f32),
            pltpu.VMEM((pool, 2 * steps, in_cols // 2), f32),
            pltpu.VMEM((q_rows, slots), f32),
            pltpu.VMEM((q_rows, head), bf16),
            pltpu.VMEM((pool, q_rows, head), bf16),
            pltpu.VMEM((tokens, o_rows), bf16),
            pltpu.VMEM((tokens, o_cols), f32),
            pltpu.VMEM((tensor, tokens, share), f32),
            pltpu.VMEM((tensor, tokens, share), bf16),
            pltpu.SemaphoreType.DMA((6,)),
            pltpu.SemaphoreType.DMA((7 + q_parts,)),
            pltpu.SemaphoreType.DMA((10 + q_parts, pool)),
            pltpu.SemaphoreType.DMA((10 + q_parts, pool)),
            pltpu.SemaphoreType.DMA((2 + 2 * pool, tensor)),
            pltpu.SemaphoreType.DMA((2 + 2 * pool, tensor)),
        ],
        compiler_params=pltpu.CompilerParams(
            collective_id=0, has_side_effects=True, vmem_limit_bytes=56 * 1024 * 1024
        ),
    )(
        hidden.reshape(steps, hidden.shape[2]),
        gain.reshape(-1, 128),
        jnp.asarray(freq),
        lengths,
        wq,
        wk,
        wv,
        wo,
        aq.T,
        bq,
        ak.T,
        bk,
        av.T,
        bv,
        ao.T,
        bo,
        keys.reshape(slots, head),
        vals.reshape(slots, head),
    )
    return out


def solution(mesh):
    in_specs = (
        P(None, ("groups", "pool"), None),
        P(),
        P("pool", "tensor"),
        P("pool", "tensor"),
        P("pool", "tensor"),
        P("tensor", "pool"),
        P("groups", "pool"),
        P(("groups", "pool"), None),
        P("groups", "pool"),
        P(("groups", "pool"), None),
        P("groups", "pool"),
        P(("groups", "pool"), None),
        P("groups", "pool"),
        P(("groups", "pool"), None),
        P(("groups", "pool"), None, "tensor", None),
        P(("groups", "pool"), None, "tensor", None),
        P(("groups", "pool")),
    )
    out_specs = P(None, "groups", "pool")
    return jax.shard_map(
        functools.partial(on_device_fused, mesh.shape["pool"], mesh.shape["tensor"]),
        mesh=mesh,
        in_specs=in_specs,
        out_specs=out_specs,
        check_vma=False,
    )
```

```python
import functools
import math

import jax
import jax.numpy as jnp
import numpy as np
from jax import lax
from jax.experimental import pallas as pl
from jax.experimental.pallas import tpu as pltpu
from jax.sharding import PartitionSpec as P

rope_base = 500000.0
norm_eps = 1e-05
MESH = pl.DeviceIdType.MESH


def rotate(values, positions):
    half_dim = values.shape[-1] // 2
    frequency = rope_base ** (-(jnp.arange(half_dim).astype(jnp.float32) * 2.0 / values.shape[-1]))
    angles = positions[..., None] * frequency
    cosine = jnp.cos(angles)
    sine = jnp.sin(angles)
    first_half = values[..., :half_dim]
    second_half = values[..., half_dim:]
    return jnp.concatenate(
        [first_half * cosine - second_half * sine, second_half * cosine + first_half * sine], -1
    )


def combine_adapter_weight(weight, factor_a, factor_b):
    return (
        weight.astype(jnp.float32) + jnp.dot(factor_a, factor_b, preferred_element_type=jnp.float32)
    ).astype(jnp.bfloat16)


def attend(queries, earlier_keys, earlier_values, new_keys, new_values, lengths, query_steps):
    decoded_row_count, steps_count, heads_count, head_dim = queries.shape
    kv_count = earlier_keys.shape[2]
    group_size = heads_count // kv_count
    scale = 1.0 / jnp.sqrt(jnp.float32(head_dim))
    grouped = queries.reshape(decoded_row_count, steps_count, kv_count, group_size, head_dim)
    scores_cache = (
        jnp.einsum("rskgd,rckd->rkgsc", grouped, earlier_keys, preferred_element_type=jnp.float32)
        * scale
    )
    scores_new = (
        jnp.einsum("rskgd,rtkd->rkgst", grouped, new_keys, preferred_element_type=jnp.float32)
        * scale
    )
    seen_cache = jnp.arange(earlier_keys.shape[1])[None, :] < lengths[:, None]
    seen_new = jnp.arange(new_keys.shape[1])[None, :] <= query_steps[:, None]
    scores_cache = jnp.where(seen_cache[:, None, None, None, :], scores_cache, -1e30)
    scores_new = jnp.where(seen_new[None, None, None, :, :], scores_new, -1e30)
    top_score = jnp.maximum(
        jnp.max(scores_cache, -1, keepdims=True), jnp.max(scores_new, -1, keepdims=True)
    )
    exp_cache = jnp.exp(scores_cache - top_score)
    exp_new = jnp.exp(scores_new - top_score)
    denominator = jnp.sum(exp_cache, -1, keepdims=True) + jnp.sum(exp_new, -1, keepdims=True)
    weights_cache = (exp_cache / denominator).astype(jnp.bfloat16)
    weights_new = (exp_new / denominator).astype(jnp.bfloat16)
    mixed = jnp.einsum(
        "rkgsc,rckd->rskgd", weights_cache, earlier_values, preferred_element_type=jnp.float32
    )
    mixed = mixed + jnp.einsum(
        "rkgst,rtkd->rskgd", weights_new, new_values, preferred_element_type=jnp.float32
    )
    return mixed.reshape(decoded_row_count, steps_count, heads_count * head_dim).astype(
        jnp.bfloat16
    )


def on_device(
    incoming_hidden,
    attention_norm_gain,
    frozen_query_weight,
    frozen_key_weight,
    frozen_value_weight,
    frozen_output_weight,
    query_adapter_first,
    query_adapter_second,
    key_adapter_first,
    key_adapter_second,
    value_adapter_first,
    value_adapter_second,
    output_adapter_first,
    output_adapter_second,
    earlier_keys,
    earlier_values,
    filled_lengths,
):
    pool_index = lax.axis_index("pool")
    tensor_index = lax.axis_index("tensor")
    feature_count = frozen_query_weight.shape[0]
    query_cols = frozen_query_weight.shape[1]
    key_cols = frozen_key_weight.shape[1]
    out_rows = frozen_output_weight.shape[0]
    down_parts = (
        lax.all_gather(query_adapter_first, "pool", axis=1, tiled=True),
        lax.all_gather(key_adapter_first, "pool", axis=1, tiled=True),
        lax.all_gather(value_adapter_first, "pool", axis=1, tiled=True),
        lax.all_gather(output_adapter_first, "pool", axis=1, tiled=True),
    )
    up_parts = (
        lax.all_gather(query_adapter_second, "pool", axis=0, tiled=True),
        lax.all_gather(key_adapter_second, "pool", axis=0, tiled=True),
        lax.all_gather(value_adapter_second, "pool", axis=0, tiled=True),
        lax.all_gather(output_adapter_second, "pool", axis=0, tiled=True),
    )
    factor_aq = lax.dynamic_slice_in_dim(
        down_parts[0], pool_index * feature_count, feature_count, 0
    )
    factor_ak = lax.dynamic_slice_in_dim(
        down_parts[1], pool_index * feature_count, feature_count, 0
    )
    factor_av = lax.dynamic_slice_in_dim(
        down_parts[2], pool_index * feature_count, feature_count, 0
    )
    factor_ao = lax.dynamic_slice_in_dim(down_parts[3], tensor_index * out_rows, out_rows, 0)
    factor_bq = lax.dynamic_slice_in_dim(up_parts[0], tensor_index * query_cols, query_cols, 1)
    factor_bk = lax.dynamic_slice_in_dim(up_parts[1], tensor_index * key_cols, key_cols, 1)
    factor_bv = lax.dynamic_slice_in_dim(up_parts[2], tensor_index * key_cols, key_cols, 1)
    factor_bo = lax.dynamic_slice_in_dim(up_parts[3], pool_index * feature_count, feature_count, 1)
    merged_inner = jnp.concatenate(
        [
            combine_adapter_weight(frozen_query_weight, factor_aq, factor_bq),
            combine_adapter_weight(frozen_key_weight, factor_ak, factor_bk),
            combine_adapter_weight(frozen_value_weight, factor_av, factor_bv),
        ],
        1,
    )
    combined_output_weight = combine_adapter_weight(frozen_output_weight, factor_ao, factor_bo)
    states = incoming_hidden.astype(jnp.float32)
    normed = (
        states
        * lax.rsqrt(jnp.mean(states * states, -1, keepdims=True) + norm_eps)
        * attention_norm_gain.astype(jnp.float32)
    )
    normed = jnp.transpose(normed.astype(jnp.bfloat16), (1, 0, 2))
    rows_dev = filled_lengths.shape[0]
    steps_count = incoming_hidden.shape[0]
    kv_local = earlier_keys.shape[2]
    head_dim = earlier_keys.shape[3]
    query_local = query_cols // head_dim
    all_steps = jnp.arange(steps_count)
    spread = lax.all_to_all(normed, "pool", split_axis=2, concat_axis=0, tiled=True)
    projected = lax.psum_scatter(
        jnp.einsum("rnd,dc->rnc", spread, merged_inner, preferred_element_type=jnp.float32),
        "pool",
        scatter_dimension=0,
        tiled=True,
    )
    positions = (filled_lengths[:, None] + all_steps[None, :]).astype(jnp.float32)[:, :, None]
    query_part = projected[..., :query_cols].reshape(rows_dev, steps_count, query_local, head_dim)
    key_part = projected[..., query_cols : query_cols + key_cols].reshape(
        rows_dev, steps_count, kv_local, head_dim
    )
    value_part = projected[..., query_cols + key_cols :].reshape(
        rows_dev, steps_count, kv_local, head_dim
    )
    queries = rotate(query_part, positions).astype(jnp.bfloat16)
    fresh_keys = rotate(key_part, positions).astype(jnp.bfloat16)
    fresh_values = value_part.astype(jnp.bfloat16)
    head_rows = attend(
        queries, earlier_keys, earlier_values, fresh_keys, fresh_values, filled_lengths, all_steps
    )
    partial_out = jnp.einsum(
        "rnk,kd->nrd",
        lax.all_gather(head_rows, "pool", axis=0, tiled=True),
        combined_output_weight,
        preferred_element_type=jnp.float32,
    )
    result = lax.psum(partial_out, "tensor").astype(jnp.bfloat16)
    return result


def layer_kernel(
    pool,
    tensor,
    steps,
    kv_heads,
    q_parts,
    x_ref,
    gain_ref,
    freq_ref,
    len_ref,
    wq_hbm,
    wk_hbm,
    wv_hbm,
    wo_hbm,
    aq_hbm,
    bq_hbm,
    ak_hbm,
    bk_hbm,
    av_hbm,
    bv_hbm,
    ao_hbm,
    bo_hbm,
    keys_hbm,
    vals_hbm,
    out_ref,
    w_in,
    w_out,
    keys,
    vals,
    a_in,
    b_in,
    a_out,
    b_out,
    a_cols,
    turn,
    x_send,
    x_recv,
    x_full,
    proj,
    rs_send,
    rs_recv,
    scores,
    h_send,
    h_recv,
    h_full,
    part,
    o_recv,
    fin,
    w_sem,
    own_sem,
    send_sem,
    recv_sem,
    t_send_sem,
    t_recv_sem,
):
    f32, bf16 = jnp.float32, jnp.bfloat16
    me = lax.axis_index("pool")
    ten = lax.axis_index("tensor")
    rank = aq_hbm.shape[0]
    depth, q_cols = wq_hbm.shape
    kv_cols = wk_hbm.shape[1]
    in_cols = q_cols + 2 * kv_cols
    o_rows, o_cols = wo_hbm.shape
    head = keys_hbm.shape[1]
    q_heads = q_cols // head
    group = q_heads // kv_heads
    tokens = pool * steps

    def at_block(index, size):
        return pl.ds(pl.multiple_of(index * size, size), size)

    def peer(off, axis, size):
        here = me if axis == "pool" else ten
        return lax.rem(here + off, size), lax.rem(here + size - off, size)

    loads = [
        pltpu.make_async_copy(wq_hbm, w_in.at[:, pl.ds(0, q_cols)], w_sem.at[0]),
        pltpu.make_async_copy(wk_hbm, w_in.at[:, pl.ds(q_cols, kv_cols)], w_sem.at[1]),
        pltpu.make_async_copy(wv_hbm, w_in.at[:, pl.ds(q_cols + kv_cols, kv_cols)], w_sem.at[2]),
        pltpu.make_async_copy(wo_hbm, w_out, w_sem.at[3]),
        pltpu.make_async_copy(keys_hbm, keys, w_sem.at[4]),
        pltpu.make_async_copy(vals_hbm, vals, w_sem.at[5]),
    ]

    def pieces(dst, src, split):
        rows = at_block(src, rank)

        def shared(ref, size):
            if not split:
                return ref.at[:, at_block(dst, size)]
            return ref.at[:, at_block(dst * tensor + ten, size // tensor)]

        def lands(ref, size):
            return ref.at[rows, at_block(ten, size // tensor) if split else pl.ds(0, size)]

        part = q_cols // q_parts
        listed = [
            (shared(aq_hbm, depth), lands(a_in.at[0], depth)),
            (shared(ak_hbm, depth), lands(a_in.at[1], depth)),
            (shared(av_hbm, depth), lands(a_in.at[2], depth)),
            (bk_hbm.at[:, at_block(ten, kv_cols)], b_in.at[rows, pl.ds(q_cols, kv_cols)]),
            (
                bv_hbm.at[:, at_block(ten, kv_cols)],
                b_in.at[rows, pl.ds(q_cols + kv_cols, kv_cols)],
            ),
            (ao_hbm.at[:, at_block(ten, o_rows)], a_out.at[rows, :]),
            (shared(bo_hbm, o_cols), lands(b_out, o_cols)),
        ]
        for i in range(q_parts):
            listed.append(
                (
                    bq_hbm.at[:, at_block(ten * q_parts + i, part)],
                    b_in.at[rows, pl.ds(i * part, part)],
                )
            )
        return listed

    own = [
        pltpu.make_async_copy(src, dst, own_sem.at[i])
        for i, (src, dst) in enumerate(pieces(me, me, False))
    ]
    shares_a, shares_b = (0, 1, 2), 6
    x_kind = 7 + q_parts
    for copy in own[:5] + own[7:]:
        copy.start()

    barrier = pltpu.get_barrier_semaphore()
    for off in range(1, pool):
        pl.semaphore_signal(
            barrier, inc=1, device_id={"pool": peer(off, "pool", pool)[0]}, device_id_type=MESH
        )
    for off in range(1, tensor):
        pl.semaphore_signal(
            barrier,
            inc=1,
            device_id={"tensor": peer(off, "tensor", tensor)[0]},
            device_id_type=MESH,
        )

    def to_pool(kind, off, src, dst_ref):
        return pltpu.make_async_remote_copy(
            src_ref=src,
            dst_ref=dst_ref,
            send_sem=send_sem.at[kind, off],
            recv_sem=recv_sem.at[kind, off],
            device_id={"pool": peer(off, "pool", pool)[0]},
            device_id_type=MESH,
        )

    def sends(off):
        dst, _ = peer(off, "pool", pool)
        out = [to_pool(i, off, a, b) for i, (a, b) in enumerate(pieces(dst, me, True))]
        return out + [to_pool(x_kind, off, x_send.at[dst], x_recv.at[me])]

    def arrivals(off):
        _, src = peer(off, "pool", pool)
        out = [to_pool(i, off, b, b) for i, (a, b) in enumerate(pieces(me, src, True))]
        return out + [to_pool(x_kind, off, x_recv.at[src], x_recv.at[src])]

    offs = list(range(1, pool))
    sent = {off: sends(off) for off in offs}
    come = {off: arrivals(off) for off in offs}
    pl.semaphore_wait(barrier, pool + tensor - 2)
    for kind in shares_a:
        for off in offs:
            sent[off][kind].start()

    fold = 16 // steps
    gain = gain_ref[...].astype(f32)
    gain = jnp.concatenate([gain[i : i + 1] for i in range(gain.shape[0])], 1)
    states = x_ref[...].astype(f32)
    mean = jnp.mean(states * states, -1, keepdims=True)
    normed = states * lax.rsqrt(mean + norm_eps) * gain
    width = depth // fold
    for dst in range(pool):
        folded = jnp.concatenate(
            [normed[:, dst * depth + i * width : dst * depth + (i + 1) * width] for i in range(fold)],
            0,
        )
        x_send[dst] = folded.astype(bf16)
    for kind in (x_kind, 3, 4) + tuple(range(7, 7 + q_parts)):
        for off in offs:
            sent[off][kind].start()
    for copy in loads[:3]:
        copy.start()

    def wait_kinds(kinds):
        for kind in kinds:
            if kind < x_kind:
                own[kind].wait()
            if kind not in (0, 1, 2, 6):
                for off in offs:
                    come[off][kind].wait_recv()

    def to_tensor(kind, off, src, dst_ref):
        return pltpu.make_async_remote_copy(
            src_ref=src,
            dst_ref=dst_ref,
            send_sem=t_send_sem.at[kind, off],
            recv_sem=t_recv_sem.at[kind, off],
            device_id={"tensor": peer(off, "tensor", tensor)[0]},
            device_id_type=MESH,
        )

    t_offs = list(range(1, tensor))
    forwarded, forwards_come = [], [[], []]

    def forward(slot, buffer, kinds):
        for off in offs:
            _, src = peer(off, "pool", pool)
            for kind in kinds:
                come[off][kind].wait_recv()
            for t_off in t_offs:
                _, t_src = peer(t_off, "tensor", tensor)
                kind = 2 + slot * pool + off

                def part_of(owner):
                    columns = at_block(owner, buffer.shape[-1] // tensor)
                    if len(buffer.shape) == 3:
                        return buffer.at[:, at_block(src, rank), columns]
                    return buffer.at[at_block(src, rank), columns]

                copy = to_tensor(kind, t_off, part_of(ten), part_of(ten))
                copy.start()
                forwarded.append(copy)
                forwards_come[slot].append(
                    to_tensor(kind, t_off, part_of(t_src), part_of(t_src))
                )

    forward(0, a_in, shares_a)
    for copy in loads[3:] + own[5:7]:
        copy.start()
    for kind in (5, 6):
        for off in offs:
            sent[off][kind].start()


    length = len_ref[0]
    lanes = freq_ref.shape[1]
    spare = freq_ref.shape[0]
    step_of = lax.rem(lax.broadcasted_iota(jnp.int32, (spare, lanes), 0), steps)
    angles = (length + step_of).astype(f32) * freq_ref[...]
    lane = lax.broadcasted_iota(jnp.int32, (spare, lanes), 1)
    turn[0] = jnp.cos(angles)
    turn[1] = jnp.where(lane < head // 2, -jnp.sin(angles), jnp.sin(angles))

    x_recv[me] = x_send[me]
    wait_kinds((x_kind,))
    rows = []
    for src in range(pool):
        got = x_recv[src].astype(f32)
        rows.append(
            jnp.concatenate([got[i * steps : (i + 1) * steps, :] for i in range(fold)], 1)
        )
    x_full[...] = jnp.concatenate(rows, 0).astype(bf16)

    tile = 256
    chunk = min(512, depth)

    def merged(a_tall, row0, b_ref, w_ref, column):
        low_rank = jnp.dot(
            a_tall[pl.ds(row0, chunk), :], b_ref[:, column], preferred_element_type=f32
        )
        return (w_ref[pl.ds(row0, chunk), column].astype(f32) + low_rank).astype(bf16)

    def project(which, first, count):
        def one(j, carry):
            column = pl.ds(pl.multiple_of(first + j * tile, tile), tile)
            total = jnp.zeros((tokens, tile), f32)
            for row0 in range(0, depth, chunk):
                block = merged(a_cols.at[which], row0, b_in, w_in, column)
                total += jnp.dot(
                    x_full[:, row0 : row0 + chunk], block, preferred_element_type=f32
                )
            proj[:, column] = total
            return carry

        lax.fori_loop(0, count // tile, one, 0)

    for copy in forwards_come[0]:
        copy.wait_recv()
    wait_kinds(shares_a)
    for which in range(3):
        a_cols[which] = a_in[which].T
    wait_kinds((3, 4))
    for load in loads[:3]:
        load.wait()
    project(1, q_cols, kv_cols)
    project(2, q_cols + kv_cols, kv_cols)
    for i in range(q_parts):
        wait_kinds((7 + i,))
        project(0, i * (q_cols // q_parts), q_cols // q_parts)

    half = in_cols // 2
    for dst in range(pool):
        mine = proj[dst * steps : (dst + 1) * steps, :]
        rs_send[dst] = jnp.concatenate([mine[:, :half], mine[:, half:]], 0)
    rs_sent, rs_come = [], []
    for off in offs:
        dst, src = peer(off, "pool", pool)
        copy = to_pool(x_kind + 1, off, rs_send.at[dst], rs_recv.at[me])
        copy.start()
        rs_sent.append(copy)
        rs_come.append(to_pool(x_kind + 1, off, rs_recv.at[src], rs_recv.at[src]))
    rs_recv[me] = rs_send[me]

    for copy in rs_come:
        copy.wait_recv()
    summed = rs_recv[0]
    for src in range(1, pool):
        summed = summed + rs_recv[src]
    flat = jnp.concatenate([summed[:steps], summed[steps:]], 1)

    def stack(first, count):
        return jnp.concatenate(
            [flat[:, first + h * head : first + (h + 1) * head] for h in range(count)], 0
        )

    def turned(values):
        turns = values.shape[0] // spare
        cos_all = jnp.concatenate([turn[0]] * turns, 0)
        sin_all = jnp.concatenate([turn[1]] * turns, 0)
        return (values * cos_all + pltpu.roll(values, head // 2, 1) * sin_all).astype(bf16)

    queries = turned(stack(0, q_heads))
    fresh_keys = turned(stack(q_cols, kv_heads))
    fresh_values = stack(q_cols + kv_cols, kv_heads).astype(bf16)

    scale = 1.0 / math.sqrt(head)
    q_rows = q_heads * steps
    span = 1024
    spans = keys.shape[0] // span
    row_head = lax.broadcasted_iota(jnp.int32, (q_rows, 1), 0) // (group * steps)
    row_step = lax.rem(lax.broadcasted_iota(jnp.int32, (q_rows, 1), 0), steps)
    nt = (((1,), (1,)), ((), ()))
    fresh_col = lax.broadcasted_iota(jnp.int32, (1, kv_heads * steps), 1)
    fresh_seen = (fresh_col // steps == row_head) & (lax.rem(fresh_col, steps) <= row_step)
    fresh_scores = jnp.where(
        fresh_seen,
        lax.dot_general(queries, fresh_keys, nt, preferred_element_type=f32) * scale,
        -1e30,
    )
    loads[4].wait()

    def score(j, top):
        at = pl.ds(pl.multiple_of(j * span, span), span)
        column = lax.broadcasted_iota(jnp.int32, (1, span), 1) + j * span
        slot = column // kv_heads
        slot_head = jnp.where(slot < length, lax.rem(column, kv_heads), -1)
        value = lax.dot_general(queries, keys[at, :], nt, preferred_element_type=f32) * scale
        value = jnp.where(slot_head == row_head, value, -1e30)
        scores[:, at] = value
        for i in range(0, span, 128):
            top = jnp.maximum(top, value[:, i : i + 128])
        return top

    top = lax.fori_loop(0, spans, score, jnp.full((q_rows, 128), -1e30, f32))
    top = jnp.maximum(
        jnp.max(top, 1, keepdims=True), jnp.max(fresh_scores, 1, keepdims=True)
    )

    def expo(j, total):
        at = pl.ds(pl.multiple_of(j * span, span), span)
        value = jnp.exp(scores[:, at] - top)
        scores[:, at] = value
        for i in range(0, span, 128):
            total = total + value[:, i : i + 128]
        return total

    total = lax.fori_loop(0, spans, expo, jnp.zeros((q_rows, 128), f32))
    fresh_exp = jnp.exp(fresh_scores - top)
    inverse = 1.0 / (
        jnp.sum(total, 1, keepdims=True) + jnp.sum(fresh_exp, 1, keepdims=True)
    )
    loads[5].wait()

    def mix(j, acc):
        at = pl.ds(pl.multiple_of(j * span, span), span)
        weights = (scores[:, at] * inverse).astype(bf16)
        return acc + jnp.dot(weights, vals[at, :], preferred_element_type=f32)

    mixed = jnp.dot(
        (fresh_exp * inverse).astype(bf16), fresh_values, preferred_element_type=f32
    )
    mixed = lax.fori_loop(0, spans, mix, mixed)
    h_send[...] = mixed.astype(bf16)

    h_sent, h_come = [], []
    for off in offs:
        _, src = peer(off, "pool", pool)
        copy = to_pool(x_kind + 2, off, h_send, h_recv.at[me])
        copy.start()
        h_sent.append(copy)
        h_come.append(to_pool(x_kind + 2, off, h_recv.at[src], h_recv.at[src]))
    h_recv[me] = h_send[...]
    forward(1, b_out, (6,))
    wait_kinds((5, 6))
    for copy in forwards_come[1]:
        copy.wait_recv()
    loads[3].wait()
    a_cols[0] = a_out[...].T

    def merge_out(j, carry):
        column = pl.ds(pl.multiple_of(j * tile, tile), tile)
        for row0 in range(0, o_rows, chunk):
            w_out[pl.ds(row0, chunk), column] = merged(a_cols.at[0], row0, b_out, w_out, column)
        return carry

    lax.fori_loop(0, o_cols // tile, merge_out, 0)

    for copy in h_come:
        copy.wait_recv()
    every = [h_recv[src].astype(f32) for src in range(pool)]
    for h in range(q_heads):
        h_full[:, h * head : (h + 1) * head] = jnp.concatenate(
            [rows_of[h * steps : (h + 1) * steps] for rows_of in every], 0
        ).astype(bf16)

    def output(j, carry):
        column = pl.ds(pl.multiple_of(j * tile, tile), tile)
        part[:, column] = jnp.dot(h_full[...], w_out[:, column], preferred_element_type=f32)
        return carry

    lax.fori_loop(0, o_cols // tile, output, 0)

    share = o_cols // tensor

    o_sent, o_come = [], []
    for off in t_offs:
        dst, src = peer(off, "tensor", tensor)
        copy = to_tensor(0, off, part.at[:, at_block(dst, share)], o_recv.at[ten])
        copy.start()
        o_sent.append(copy)
        o_come.append(to_tensor(0, off, o_recv.at[src], o_recv.at[src]))
    o_recv[ten] = part[:, at_block(ten, share)]
    for copy in o_come:
        copy.wait_recv()
    done = o_recv[0]
    for src in range(1, tensor):
        done = done + o_recv[src]
    done = jnp.concatenate(
        [done[r * steps + s : r * steps + s + 1] for s in range(steps) for r in range(pool)], 0
    )
    fin[ten] = done.astype(bf16)
    f_sent, f_come = [], []
    for off in t_offs:
        _, src = peer(off, "tensor", tensor)
        copy = to_tensor(1, off, fin.at[ten], fin.at[ten])
        copy.start()
        f_sent.append(copy)
        f_come.append(to_tensor(1, off, fin.at[src], fin.at[src]))
    for copy in f_come:
        copy.wait_recv()
    for src in range(tensor):
        block = fin[src].astype(f32)
        for s in range(steps):
            out_ref[s, :, src * share : (src + 1) * share] = block[
                s * pool : (s + 1) * pool
            ].astype(bf16)
    for off in offs:
        for copy in sent[off]:
            copy.wait_send()
    for copy in forwarded + rs_sent + h_sent + o_sent + f_sent:
        copy.wait_send()


def fits(pool, tensor, args):
    hidden, wq, wk, wo = args[0], args[2], args[3], args[5]
    rank, keys = args[7].shape[0], args[14]
    steps = hidden.shape[0]
    return (
        keys.shape[0] == 1
        and keys.shape[3] == 128
        and rank % 16 == 0
        and pool > 1
        and tensor > 1
        and pool * steps == 16
        and steps == 4
        and (keys.shape[2] * steps) % 8 == 0
        and wq.shape[0] % 512 == 0
        and wq.shape[1] % 256 == 0
        and wk.shape[1] % 256 == 0
        and wo.shape[0] == wq.shape[0]
        and wo.shape[1] % (128 * tensor) == 0
        and wo.shape[1] % 256 == 0
        and wq.shape[0] % (128 * tensor) == 0
        and hidden.shape[2] % 128 == 0
        and (keys.shape[1] * keys.shape[2]) % 1024 == 0
        and wq.shape[0] * (wq.shape[1] + 2 * wk.shape[1] + wo.shape[1]) <= 12 * 1024 * 1024
    )


def on_device_fused(pool, tensor, *args):
    if not fits(pool, tensor, args):
        return on_device(*args)
    f32, bf16 = jnp.float32, jnp.bfloat16
    hidden, gain, wq, wk, wv, wo, aq, bq, ak, bk, av, bv, ao, bo, keys, vals, lengths = args
    steps = hidden.shape[0]
    kv_heads, head = keys.shape[2:]
    rank = bq.shape[0]
    depth, q_cols = wq.shape
    in_cols = q_cols + 2 * wk.shape[1]
    o_rows, o_cols = wo.shape
    q_rows = q_cols // head * steps
    slots = keys.shape[1] * kv_heads
    tokens = pool * steps
    frequency = rope_base ** (-(np.arange(head // 2) * 2.0 / head))
    freq = np.broadcast_to(np.tile(frequency, 2)[None, :], (8, head)).astype(np.float32)
    vmem = pl.BlockSpec(memory_space=pltpu.VMEM)
    hbm = pl.BlockSpec(memory_space=pl.ANY)
    share = o_cols // tensor
    q_parts = math.gcd(q_cols // 256, 4)
    out = pl.pallas_call(
        functools.partial(layer_kernel, pool, tensor, steps, kv_heads, q_parts),
        out_shape=jax.ShapeDtypeStruct((steps, pool, o_cols), bf16),
        in_specs=[vmem, vmem, vmem, pl.BlockSpec(memory_space=pltpu.SMEM)] + [hbm] * 14,
        out_specs=vmem,
        scratch_shapes=[
            pltpu.VMEM((depth, in_cols), bf16),
            pltpu.VMEM((o_rows, o_cols), bf16),
            pltpu.VMEM((slots, head), bf16),
            pltpu.VMEM((slots, head), bf16),
            pltpu.VMEM((3, pool * rank, depth), bf16),
            pltpu.VMEM((pool * rank, in_cols), bf16),
            pltpu.VMEM((pool * rank, o_rows), bf16),
            pltpu.VMEM((pool * rank, o_cols), bf16),
            pltpu.VMEM((3, depth, pool * rank), bf16),
            pltpu.VMEM((2, 8, head), f32),
            pltpu.VMEM((pool, 16, depth * steps // 16), bf16),
            pltpu.VMEM((pool, 16, depth * steps // 16), bf16),
            pltpu.VMEM((tokens, depth), bf16),
            pltpu.VMEM((tokens, in_cols), f32),
            pltpu.VMEM((pool, 2 * steps, in_cols // 2), f32),
            pltpu.VMEM((pool, 2 * steps, in_cols // 2), f32),
            pltpu.VMEM((q_rows, slots), f32),
            pltpu.VMEM((q_rows, head), bf16),
            pltpu.VMEM((pool, q_rows, head), bf16),
            pltpu.VMEM((tokens, o_rows), bf16),
            pltpu.VMEM((tokens, o_cols), f32),
            pltpu.VMEM((tensor, tokens, share), f32),
            pltpu.VMEM((tensor, tokens, share), bf16),
            pltpu.SemaphoreType.DMA((6,)),
            pltpu.SemaphoreType.DMA((7 + q_parts,)),
            pltpu.SemaphoreType.DMA((10 + q_parts, pool)),
            pltpu.SemaphoreType.DMA((10 + q_parts, pool)),
            pltpu.SemaphoreType.DMA((2 + 2 * pool, tensor)),
            pltpu.SemaphoreType.DMA((2 + 2 * pool, tensor)),
        ],
        compiler_params=pltpu.CompilerParams(
            collective_id=0, has_side_effects=True, vmem_limit_bytes=56 * 1024 * 1024
        ),
    )(
        hidden.reshape(steps, hidden.shape[2]),
        gain.reshape(-1, 128),
        jnp.asarray(freq),
        lengths,
        wq,
        wk,
        wv,
        wo,
        aq.T,
        bq,
        ak.T,
        bk,
        av.T,
        bv,
        ao.T,
        bo,
        keys.reshape(slots, head),
        vals.reshape(slots, head),
    )
    return out


def solution(mesh):
    in_specs = (
        P(None, ("groups", "pool"), None),
        P(),
        P("pool", "tensor"),
        P("pool", "tensor"),
        P("pool", "tensor"),
        P("tensor", "pool"),
        P("groups", "pool"),
        P(("groups", "pool"), None),
        P("groups", "pool"),
        P(("groups", "pool"), None),
        P("groups", "pool"),
        P(("groups", "pool"), None),
        P("groups", "pool"),
        P(("groups", "pool"), None),
        P(("groups", "pool"), None, "tensor", None),
        P(("groups", "pool"), None, "tensor", None),
        P(("groups", "pool")),
    )
    out_specs = P(None, "groups", "pool")
    return jax.shard_map(
        functools.partial(on_device_fused, mesh.shape["pool"], mesh.shape["tensor"]),
        mesh=mesh,
        in_specs=in_specs,
        out_specs=out_specs,
        check_vma=False,
    )
```
